32 devices in a mesh: seq: 8 (over z, x), ch: 4 (over y, core).
Axes of the slice: x: 2, y: 2, z: 4, core: 2. Of those that a mesh axis runs over, the one named last changes fastest.
Arguments:
- signal: bfloat16 [4096, 2048], P('seq', 'ch'), may hold values from -6 to 6
- filter_raw: bfloat16 [4096, 2048], P('seq', 'ch'), may hold values from -6 to 6
- gate: bfloat16 [4096, 2048], P('seq', 'ch'), may hold values from -6 to 6
- d_out: bfloat16 [4096, 2048], P('seq', 'ch'), may hold values from -6 to 6
- w_first: bfloat16 [32, 64, 64], P('ch'), may hold values from -0.75 to 0.75
- w_second: bfloat16 [64, 32, 32], P('ch'), may hold values from -1 to 1
Outputs:
- grad_signal: bfloat16 [4096, 2048], P('seq', 'ch')
- grad_filter: bfloat16 [4096, 2048], P('seq', 'ch')
- grad_gate: bfloat16 [4096, 2048], P('seq', 'ch')
- grad_first: float32 [32, 64, 64], P('ch', 'seq')
- grad_second: float32 [64, 32, 32], P('ch', 'seq')
The draws below stay inside these ranges and needn't reach their ends.
All inputs are finite; a program needn't handle non-finite values.
Results may differ from the reference program's by a relative error of at most 0.02.
Values may be sent and summed in bfloat16 or wider, within the bound.
A program may use at most 128 MiB of HBM per device.

```python
import jax
import jax.numpy as jnp
from jax import lax

WIDTH = 2048
BLOCK = 64
BLOCKS = 32
SEQ = 4096


def steps_of(own_key, extent, shards, low, high):
    loudness = 1.0
    for dim, shards_of in shards:
        heights = jax.random.uniform(jax.random.fold_in(jax.random.fold_in(own_key, 6), dim), (shards_of,), jnp.float32, low / len(shards), high / len(shards))
        loudness = loudness * jnp.repeat(jnp.exp(heights), extent[dim] // shards_of).reshape((-1,) + (1,) * (len(extent) - 1 - dim))
    return loudness


def noise(rng, extent, width, most, split=(), kind=jnp.bfloat16):
    level = steps_of(rng, extent, split, -0.22, 0.18) if split else 1.0
    entries = jax.random.normal(rng, extent, jnp.float32) * width * level
    return jnp.minimum(jnp.maximum(entries, -most), most).astype(kind)


def setup_inputs(seed: int = 0) -> dict:
    seeds = jax.random.split(jax.random.key(seed), 7)
    return {
        "signal": noise(seeds[0], (SEQ, WIDTH), 1.0, 6.0, ((0, 8), (1, 4))),
        "filter_raw": noise(seeds[1], (SEQ, WIDTH), 1.0, 6.0, ((0, 8), (1, 4))),
        "gate": noise(seeds[2], (SEQ, WIDTH), 1.0, 6.0, ((0, 8), (1, 4))),
        "d_out": noise(seeds[3], (SEQ, WIDTH), 1.0, 6.0, ((0, 8), (1, 4))),
        "w_first": noise(seeds[4], (BLOCKS, BLOCK, BLOCK), BLOCK ** -0.5, 0.75, ((0, 4),)),
        "w_second": noise(seeds[5], (BLOCK, BLOCKS, BLOCKS), BLOCKS ** -0.5, 1.0, ((0, 4),)),
    }


def block_conv(pair):
    values, kernel = pair
    count = values.shape[0]
    length = 2 * count
    spectrum = jnp.fft.rfft(values, n=length, axis=0) * jnp.fft.rfft(kernel, n=length, axis=0)
    return jnp.fft.irfft(spectrum, n=length, axis=0)[:count]


def block_adjoint(triple):
    values, kernel, incoming = triple
    count = values.shape[0]
    length = 2 * count
    incoming_spec = jnp.fft.rfft(incoming, n=length, axis=0)
    toward_signal = jnp.fft.irfft(jnp.conj(jnp.fft.rfft(kernel, n=length, axis=0)) * incoming_spec, n=length, axis=0)[:count]
    toward_filter = jnp.fft.irfft(jnp.conj(jnp.fft.rfft(values, n=length, axis=0)) * incoming_spec, n=length, axis=0)[:count]
    return toward_signal, toward_filter


def by_blocks(array):
    return jnp.transpose(array.reshape(SEQ, BLOCKS, BLOCK), (1, 0, 2))


def from_blocks(array):
    return jnp.transpose(array, (1, 0, 2)).reshape(SEQ, WIDTH)


def reference(signal, filter_raw, gate, d_out, w_first, w_second):
    scale = float(SEQ) ** -0.5
    signal_wide = signal.astype(jnp.float32)
    kernel = filter_raw.astype(jnp.float32) * scale
    conv = from_blocks(lax.map(block_conv, (by_blocks(signal_wide), by_blocks(kernel)))).astype(jnp.bfloat16)
    gate_wide = gate.astype(jnp.float32)
    product = (conv.astype(jnp.float32) * gate_wide).astype(jnp.bfloat16)
    product_blocks = product.reshape(SEQ, BLOCKS, BLOCK).astype(jnp.float32)
    first_wide = w_first.astype(jnp.float32)
    second_wide = w_second.astype(jnp.float32)
    first_mix = jnp.einsum("tij,ijk->tik", product_blocks, first_wide).astype(jnp.bfloat16)
    incoming = d_out.reshape(SEQ, BLOCK, BLOCKS).astype(jnp.float32)
    second_back = jnp.einsum("tko,kio->tki", incoming, second_wide).astype(jnp.bfloat16)
    grad_second = jnp.einsum("tik,tko->kio", first_mix.astype(jnp.float32), incoming)
    back_wide = second_back.astype(jnp.float32)
    grad_product = jnp.einsum("tki,ijk->tij", back_wide, first_wide).reshape(SEQ, WIDTH)
    grad_first = jnp.einsum("tij,tki->ijk", product_blocks, back_wide)
    grad_gate = (grad_product * conv.astype(jnp.float32)).astype(jnp.bfloat16)
    grad_conv = grad_product * gate_wide
    toward_signal, toward_filter = lax.map(block_adjoint, (by_blocks(signal_wide), by_blocks(kernel), by_blocks(grad_conv)))
    grad_signal = from_blocks(toward_signal).astype(jnp.bfloat16)
    grad_filter = (from_blocks(toward_filter) * scale).astype(jnp.bfloat16)
    return grad_signal, grad_filter, grad_gate, grad_first, grad_second
```

```python
import math

import jax
import jax.numpy as jnp
import ml_dtypes
import numpy as np
from jax import lax
from jax.experimental import pallas as pl
from jax.experimental.pallas import tpu as pltpu
from jax.sharding import PartitionSpec as P

HIGHEST = lax.Precision.HIGHEST


def counting(count):
    return jnp.arange(count, dtype=jnp.int32)


def phase_table(row_ids, col_ids, length, sign):
    angles = (
        2.0 * math.pi / length * (row_ids[:, None] * col_ids[None, :] % length).astype(jnp.float32)
    )
    return (jnp.cos(angles), sign * jnp.sin(angles))


def contract(form, table, real_part, imag_part):
    cosine, sine = table
    out_real = jnp.einsum(form, cosine, real_part, precision=HIGHEST) - jnp.einsum(
        form, sine, imag_part, precision=HIGHEST
    )
    out_imag = jnp.einsum(form, cosine, imag_part, precision=HIGHEST) + jnp.einsum(
        form, sine, real_part, precision=HIGHEST
    )
    return (out_real, out_imag)


def rotate(cosine, sine, real_part, imag_part):
    return (real_part * cosine - imag_part * sine, real_part * sine + imag_part * cosine)


def factors(length):
    return (length // 128, 128)


def local_forward(real_part, imag_part):
    fields, group, rows, width = real_part.shape
    outer, inner = factors(rows)
    real_part = real_part.reshape(fields, group, outer, inner, width)
    imag_part = imag_part.reshape(fields, group, outer, inner, width)
    real_part, imag_part = contract(
        "qa,fkabc->fkqbc",
        phase_table(counting(outer), counting(outer), outer, -1.0),
        real_part,
        imag_part,
    )
    cosine, sine = phase_table(counting(outer), counting(inner), rows, -1.0)
    real_part, imag_part = rotate(cosine[:, :, None], sine[:, :, None], real_part, imag_part)
    return contract(
        "rb,fkqbc->fkqrc",
        phase_table(counting(inner), counting(inner), inner, -1.0),
        real_part,
        imag_part,
    )


def local_inverse(real_part, imag_part):
    fields, group, outer, inner, width = real_part.shape
    rows = outer * inner
    real_part, imag_part = contract(
        "br,fkqrc->fkqbc",
        phase_table(counting(inner), counting(inner), inner, 1.0),
        real_part,
        imag_part,
    )
    cosine, sine = phase_table(counting(outer), counting(inner), rows, 1.0)
    real_part, imag_part = rotate(cosine[:, :, None], sine[:, :, None], real_part, imag_part)
    real_part, imag_part = contract(
        "aq,fkqbc->fkabc",
        phase_table(counting(outer), counting(outer), outer, 1.0),
        real_part,
        imag_part,
    )
    return (
        real_part.reshape(fields, group, rows, width),
        imag_part.reshape(fields, group, rows, width),
    )


def forward_transform(fields):
    devices = lax.axis_size("seq")
    count, rows, width = fields.shape
    piece = rows // devices
    span = 2 * devices
    whole = span * rows
    parts = lax.all_to_all(fields[:, None], "seq", split_axis=2, concat_axis=1, tiled=True)
    cosine, sine = phase_table(counting(span), counting(devices), span, -1.0)
    real_part = jnp.einsum("ka,fabc->fkbc", cosine, parts, precision=HIGHEST)
    imag_part = jnp.einsum("ka,fabc->fkbc", sine, parts, precision=HIGHEST)
    positions = lax.axis_index("seq") * piece + counting(piece)
    cosine, sine = phase_table(counting(span), positions, whole, -1.0)
    real_part, imag_part = rotate(cosine[:, :, None], sine[:, :, None], real_part, imag_part)
    spectrum = lax.all_to_all(
        jnp.stack([real_part, imag_part], axis=1), "seq", split_axis=2, concat_axis=3, tiled=True
    )
    return local_forward(spectrum[:, 0], spectrum[:, 1])


def inverse_transform(real_part, imag_part):
    devices = lax.axis_size("seq")
    real_part, imag_part = local_inverse(real_part, imag_part)
    group = real_part.shape[1]
    rows = real_part.shape[2]
    span = 2 * devices
    whole = span * rows
    classes = lax.axis_index("seq") * group + counting(group)
    cosine, sine = phase_table(classes, counting(rows), whole, 1.0)
    real_part, imag_part = rotate(cosine[:, :, None], sine[:, :, None], real_part, imag_part)
    gathered = lax.all_to_all(
        jnp.stack([real_part, imag_part], axis=1), "seq", split_axis=3, concat_axis=2, tiled=True
    )
    cosine, sine = phase_table(counting(devices), counting(span), span, 1.0)
    inverse_scale = 1.0 / whole
    out_real = (
        jnp.einsum("ak,fkbc->fabc", cosine, gathered[:, 0], precision=HIGHEST)
        - jnp.einsum("ak,fkbc->fabc", sine, gathered[:, 1], precision=HIGHEST)
    ) * inverse_scale
    slab = lax.all_to_all(out_real, "seq", split_axis=1, concat_axis=2, tiled=True)
    return slab[:, 0]


def adjoint_spectra(spectra_real, spectra_imag, incoming_real, incoming_imag):
    toward_signal_real = spectra_real[1] * incoming_real + spectra_imag[1] * incoming_imag
    toward_signal_imag = spectra_real[1] * incoming_imag - spectra_imag[1] * incoming_real
    toward_filter_real = spectra_real[0] * incoming_real + spectra_imag[0] * incoming_imag
    toward_filter_imag = spectra_real[0] * incoming_imag - spectra_imag[0] * incoming_real
    return (toward_signal_real, toward_signal_imag, toward_filter_real, toward_filter_imag)


def shards_general(signal, filter_raw, gate, d_out, w_first, w_second):
    rows, width = signal.shape
    scale = float(rows * lax.axis_size("seq")) ** (-0.5)
    signal_wide = signal.astype(jnp.float32)
    kernel = filter_raw.astype(jnp.float32) * scale
    spectra_real, spectra_imag = forward_transform(jnp.stack([signal_wide, kernel]))
    mixed_real = spectra_real[0] * spectra_real[1] - spectra_imag[0] * spectra_imag[1]
    mixed_imag = spectra_real[0] * spectra_imag[1] + spectra_imag[0] * spectra_real[1]
    conv = inverse_transform(mixed_real[None], mixed_imag[None])[0].astype(jnp.bfloat16)
    gate_wide = gate.astype(jnp.float32)
    product = (conv.astype(jnp.float32) * gate_wide).astype(jnp.bfloat16)
    blocks = w_first.shape[0]
    block = w_first.shape[1]
    product_blocks = product.reshape(rows, blocks, block)
    first_mix = jnp.einsum(
        "tij,ijk->tik", product_blocks, w_first, preferred_element_type=jnp.float32
    ).astype(jnp.bfloat16)
    received = lax.all_to_all(first_mix, "ch", split_axis=2, concat_axis=1, tiled=True)
    incoming = d_out.reshape(rows, w_second.shape[0], w_second.shape[1])
    second_back = jnp.einsum(
        "tko,kio->tki", incoming, w_second, preferred_element_type=jnp.float32
    ).astype(jnp.bfloat16)
    grad_second = jnp.einsum("tik,tko->kio", received, incoming, preferred_element_type=jnp.float32)
    returned = lax.all_to_all(second_back, "ch", split_axis=2, concat_axis=1, tiled=True)
    grad_product = jnp.einsum(
        "tki,ijk->tij", returned, w_first, preferred_element_type=jnp.float32
    ).reshape(rows, width)
    grad_first = jnp.einsum(
        "tij,tki->ijk", product_blocks, returned, preferred_element_type=jnp.float32
    )
    grad_gate = (grad_product * conv.astype(jnp.float32)).astype(jnp.bfloat16)
    grad_conv = grad_product * gate_wide
    incoming_real, incoming_imag = forward_transform(grad_conv[None])
    sig_real, sig_imag, fil_real, fil_imag = adjoint_spectra(
        spectra_real, spectra_imag, incoming_real[0], incoming_imag[0]
    )
    results = inverse_transform(jnp.stack([sig_real, fil_real]), jnp.stack([sig_imag, fil_imag]))
    grad_signal = results[0].astype(jnp.bfloat16)
    grad_filter = (results[1] * scale).astype(jnp.bfloat16)
    grad_first = lax.psum_scatter(
        grad_first.astype(jnp.bfloat16), "seq", scatter_dimension=1, tiled=True
    ).astype(jnp.float32)
    grad_second = lax.psum_scatter(grad_second, "seq", scatter_dimension=1, tiled=True)
    return (grad_signal, grad_filter, grad_gate, grad_first, grad_second)


F32 = jnp.float32
BF16 = jnp.bfloat16
LANES = 128
HALF = 64
INNER = 128
CHUNK = 16


def dft_tables(outer, scale):
    length = outer * INNER
    q = np.arange(outer // 2 + 1)[:, None, None]
    r = np.arange(INNER)[None, :, None]
    b = np.arange(INNER)[None, None, :]
    angle = 2.0 * np.pi / length * ((b * (q + outer * r)) % length)
    c, s = np.cos(angle), np.sin(angle)
    forward = np.concatenate(
        [np.concatenate([c, s], axis=2), np.concatenate([-s, c], axis=2)], axis=1
    )
    inverse = forward.transpose(0, 2, 1) * (scale / length)
    return forward.astype(ml_dtypes.bfloat16), inverse.astype(ml_dtypes.bfloat16)


def times(value, cosine, sine):
    real, imag = value
    if imag is None:
        return (real * cosine, real * sine)
    return (real * cosine - imag * sine, real * sine + imag * cosine)


def real_dft(values, length):
    if length == 2:
        return [(values[0], None), (values[0], None)]
    even = real_dft(values[0::2], length // 2)
    odd = real_dft(values[1::2], length // 2)
    half, quarter = length // 2, length // 4
    out = [None] * (half + 1)
    for q in range(quarter + 1):
        er, ei = even[q]
        if q == 0:
            out[0] = (er + odd[0][0], None)
            out[half] = (er - odd[0][0], None)
        elif q == quarter:
            out[q] = (er, -odd[q][0])
        else:
            angle = 2.0 * math.pi * q / length
            tr, ti = times(odd[q], math.cos(angle), -math.sin(angle))
            out[q] = (er + tr, ei + ti)
            out[half - q] = (er - tr, ti - ei)
    return out


def real_inverse(values, length):
    if length == 2:
        return [values[0][0] + values[1][0]]
    half, quarter = length // 2, length // 4
    even, odd = [], []
    for q in range(quarter + 1):
        zr, zi = values[q]
        if q == 0:
            wr = values[half][0]
            even.append((zr + wr, None))
            odd.append((zr - wr, None))
        elif q == quarter:
            even.append((zr + zr, None))
            odd.append((-(zi + zi), None))
        else:
            wr, wi = values[half - q]
            even.append((zr + wr, zi - wi))
            angle = 2.0 * math.pi * q / length
            odd.append(times((zr - wr, zi + wi), math.cos(angle), math.sin(angle)))
    out = [None] * half
    out[0::2] = real_inverse(even, half)
    out[1::2] = real_inverse(odd, half)
    return out


def low_lanes(rows):
    return lax.broadcasted_iota(jnp.int32, (rows, LANES), 1) < HALF


def swap(value):
    return pltpu.roll(value, HALF, 1)


def store_classes(y_ref, rows, spectrum):
    for q, (real, imag) in enumerate(spectrum):
        y_ref[q, pl.ds(rows, CHUNK), :] = real.astype(BF16)
        imag = jnp.zeros_like(real) if imag is None else imag
        y_ref[q, pl.ds(INNER + rows, CHUNK), :] = imag.astype(BF16)


def load_classes(z_ref, rows, classes):
    out = []
    for q in range(classes):
        real = z_ref[q, pl.ds(rows, CHUNK), :]
        edge = q == 0 or q == classes - 1
        out.append((real, None if edge else z_ref[q, pl.ds(INNER + rows, CHUNK), :]))
    return out


def pack_kernel(signal_ref, filter_ref, out_ref):
    rows = signal_ref.shape[0]
    low = low_lanes(rows)
    for p in range(out_ref.shape[0] // 2):
        cols = slice(p * LANES, (p + 1) * LANES)
        a = signal_ref[:, cols].astype(F32)
        b = filter_ref[:, cols].astype(F32)
        out_ref[2 * p] = jnp.where(low, a, swap(b)).astype(BF16)
        out_ref[2 * p + 1] = jnp.where(low, swap(a), b).astype(BF16)


def unpack_kernel(in_ref, signal_ref, filter_ref):
    rows = signal_ref.shape[0]
    low = low_lanes(rows)
    for p in range(in_ref.shape[0] // 2):
        cols = slice(p * LANES, (p + 1) * LANES)
        a = in_ref[2 * p].astype(F32)
        b = in_ref[2 * p + 1].astype(F32)
        filter_ref[:, cols] = jnp.where(low, a, swap(b)).astype(BF16)
        signal_ref[:, cols] = jnp.where(low, swap(a), b).astype(BF16)


def conv_kernel(pair_ref, forward_ref, inverse_ref, spec_ref, conv_ref, y_ref, z_ref):
    devices, rows, _ = pair_ref.shape
    classes = forward_ref.shape[0]
    outer = 2 * (classes - 1)
    tiles = rows // INNER

    def first(j, carry):
        at = pl.multiple_of(j * CHUNK, CHUNK)
        points = [
            pair_ref[a // tiles, pl.ds((a % tiles) * INNER + at, CHUNK), :].astype(F32)
            for a in range(outer // 2)
        ]
        store_classes(y_ref, at, real_dft(points, outer))
        return carry

    lax.fori_loop(0, INNER // CHUNK, first, 0)

    def middle(q, carry):
        x = jnp.dot(forward_ref[q], y_ref[q], preferred_element_type=F32)
        spec_ref[q] = x.astype(BF16)
        o = swap(x)
        xr, xi, orr, oi = x[:INNER], x[INNER:], o[:INNER], o[INNER:]
        mixed = jnp.concatenate([xr * orr - xi * oi, xr * oi + xi * orr], axis=0)
        z_ref[q] = jnp.dot(inverse_ref[q], mixed.astype(BF16), preferred_element_type=F32)
        return carry

    lax.fori_loop(0, classes, middle, 0, unroll=3)
    low = low_lanes(CHUNK)
    halves = tiles // 2

    def last(j, carry):
        at = pl.multiple_of(j * CHUNK, CHUNK)
        points = real_inverse(load_classes(z_ref, at, classes), outer)
        for s in range(devices):
            for m in range(halves):
                a = s * tiles + m
                value = jnp.where(low, points[a], points[a + halves])
                conv_ref[s, pl.ds(m * INNER + at, CHUNK), :] = value.astype(BF16)
        return carry

    lax.fori_loop(0, INNER // CHUNK, last, 0)


def adjoint_kernel(grad_ref, spec_ref, forward_ref, inverse_ref, out_ref, y_ref, z_ref):
    devices, packed, _ = grad_ref.shape
    classes = forward_ref.shape[0]
    outer = 2 * (classes - 1)
    halves = packed // INNER
    tiles = 2 * halves
    low = low_lanes(CHUNK)

    def first(j, carry):
        at = pl.multiple_of(j * CHUNK, CHUNK)
        points = [None] * (outer // 2)
        for s in range(devices):
            for m in range(halves):
                value = grad_ref[s, pl.ds(m * INNER + at, CHUNK), :].astype(F32)
                other = swap(value)
                points[s * tiles + m] = jnp.where(low, value, other)
                points[s * tiles + halves + m] = jnp.where(low, other, value)
        store_classes(y_ref, at, real_dft(points, outer))
        return carry

    lax.fori_loop(0, INNER // CHUNK, first, 0)

    def middle(q, carry):
        g = jnp.dot(forward_ref[q], y_ref[q], preferred_element_type=F32)
        x = spec_ref[q].astype(F32)
        gr, gi, xr, xi = g[:INNER], g[INNER:], x[:INNER], x[INNER:]
        mixed = jnp.concatenate([xr * gr + xi * gi, xr * gi - xi * gr], axis=0)
        z_ref[q] = jnp.dot(inverse_ref[q], mixed.astype(BF16), preferred_element_type=F32)
        return carry

    lax.fori_loop(0, classes, middle, 0, unroll=3)

    def last(j, carry):
        at = pl.multiple_of(j * CHUNK, CHUNK)
        points = real_inverse(load_classes(z_ref, at, classes), outer)
        for a in range(outer // 2):
            out_ref[a // tiles, pl.ds((a % tiles) * INNER + at, CHUNK), :] = points[a].astype(BF16)
        return carry

    lax.fori_loop(0, INNER // CHUNK, last, 0)


def back_kernel(d_out_ref, second_ref, out_ref):
    value = jnp.dot(d_out_ref[...], second_ref[...], preferred_element_type=F32).astype(BF16)
    for c in range(out_ref.shape[0]):
        out_ref[c] = value[:, c * LANES : (c + 1) * LANES]


def joined(ref):
    return jnp.concatenate([ref[c] for c in range(ref.shape[0])], axis=1)


def grad_product_of(back, first):
    return lax.dot_general(back, first, (((1,), (1,)), ((), ())), preferred_element_type=F32)


def grad_conv_kernel(back_ref, first_ref, gate_ref, out_ref):
    value = grad_product_of(joined(back_ref), first_ref[...]) * gate_ref[...].astype(F32)
    half = value.shape[0] // 2
    low = low_lanes(half)
    for p in range(out_ref.shape[0] // 2):
        top = value[:half, p * LANES : (p + 1) * LANES]
        bottom = value[half:, p * LANES : (p + 1) * LANES]
        out_ref[2 * p] = jnp.where(low, top, swap(bottom)).astype(BF16)
        out_ref[2 * p + 1] = jnp.where(low, swap(top), bottom).astype(BF16)


def mix_kernel(conv_ref, back_ref, first_ref, gate_ref, mix_ref, grad_gate_ref, grad_first_ref):
    devices, half, _ = conv_ref.shape
    low = low_lanes(half)
    parts = []
    for p in range(devices // 2):
        a = conv_ref[2 * p].astype(F32)
        b = conv_ref[2 * p + 1].astype(F32)
        parts.append(
            jnp.concatenate([jnp.where(low, a, swap(b)), jnp.where(low, swap(a), b)], axis=0)
        )
    conv = jnp.concatenate(parts, axis=1)
    product = (conv * gate_ref[...].astype(F32)).astype(BF16)
    first = first_ref[...]
    mix = jnp.dot(product, first, preferred_element_type=F32).astype(BF16)
    groups = mix_ref.shape[0]
    for c in range(groups):
        mix_ref[c] = mix[:, c * LANES : (c + 1) * LANES]
    back = joined(back_ref)
    grad_gate_ref[...] = (grad_product_of(back, first) * conv).astype(BF16)
    whole = lax.dot_general(product, back, (((0,), (0,)), ((), ())), preferred_element_type=F32)
    count = whole.shape[0]
    lane = lax.broadcasted_iota(jnp.int32, (count, LANES), 1)
    row = lax.broadcasted_iota(jnp.int32, (count, LANES), 0)
    inner = LANES // devices
    keep = lane // inner == row // (count // devices)
    grads = jnp.zeros((count, LANES), F32)
    for c in range(groups):
        value = jnp.where(keep, whole[:, c * LANES : (c + 1) * LANES], 0.0)
        shift = inner
        while shift < LANES:
            value = value + pltpu.roll(value, shift, 1)
            shift *= 2
        grads = jnp.where((lane // inner) % groups == c, value, grads)
    block = count // devices
    piece = block // devices
    pairs = devices // 2
    small = low_lanes(piece)
    for i in range(pairs):
        for s in range(devices):
            a = grads[i * block + s * piece : i * block + (s + 1) * piece]
            k = i + pairs
            b = grads[k * block + s * piece : k * block + (s + 1) * piece]
            grad_first_ref[s, i * piece : (i + 1) * piece, :] = jnp.where(small, a, b)


def second_kernel(mix_ref, d_out_ref, grad_first_ref, out_ref, inner, width):
    groups = mix_ref.shape[0]
    devices, first_rows, _ = grad_first_ref.shape
    out_ref[:, :first_rows, :] = grad_first_ref[...]
    d_out = d_out_ref[...]
    lane = lax.broadcasted_iota(jnp.int32, (LANES, LANES), 1)
    row = lax.broadcasted_iota(jnp.int32, (LANES, LANES), 0)
    folds = LANES // width
    per = devices // groups
    slot = lax.broadcasted_iota(jnp.int32, (inner, LANES), 1) // width
    for c in range(groups):
        whole = lax.dot_general(
            mix_ref[c], d_out, (((0,), (0,)), ((), ())), preferred_element_type=F32
        )
        total = jnp.zeros((LANES, LANES), F32)
        for g in range(whole.shape[1] // LANES):
            keep = lane // width + g * folds == row % inner
            total = total + jnp.where(keep, whole[:, g * LANES : (g + 1) * LANES], 0.0)
        shift = width
        while shift < LANES:
            total = total + pltpu.roll(total, shift, 1)
            shift *= 2
        for d in range(per):
            base = d * folds * inner
            piece = jnp.zeros((inner, LANES), F32)
            for i in range(folds):
                piece = jnp.where(slot == i, total[base + i * inner : base + (i + 1) * inner], piece)
            out_ref[c * per + d, first_rows:, :] = piece


def call(kernel, outs, scratch=(), flops=0, moved=0):
    return pl.pallas_call(
        kernel,
        out_shape=outs,
        scratch_shapes=list(scratch),
        compiler_params=pltpu.CompilerParams(vmem_limit_bytes=48 * 1024 * 1024),
        cost_estimate=pl.CostEstimate(flops=flops, bytes_accessed=moved, transcendentals=0),
    )


def exchange(value, axis):
    return lax.all_to_all(value, axis, split_axis=0, concat_axis=0, tiled=True)


def shards_whole(signal, filter_raw, gate, d_out, w_first, w_second):
    rows, width = signal.shape
    devices = lax.axis_size("seq")
    groups = lax.axis_size("ch")
    length = rows * devices
    outer = 2 * length // INNER
    classes = outer // 2 + 1
    forward, inverse = (jnp.asarray(t) for t in dft_tables(outer, float(length) ** (-0.5)))
    blocks, block, _ = w_first.shape
    inner, across, out_block = w_second.shape
    shape = jax.ShapeDtypeStruct
    scratch = (
        pltpu.VMEM((classes, 2 * INNER, LANES), BF16),
        pltpu.VMEM((classes, 2 * INNER, LANES), F32),
    )

    second_t = w_second.transpose(0, 2, 1).reshape(inner, out_block, groups, blocks, 1)
    second = jnp.where(
        jnp.eye(inner, dtype=bool)[:, None, None, None, :], second_t, jnp.zeros((), BF16)
    ).reshape(width, width)
    first = jnp.where(
        jnp.eye(blocks, dtype=bool)[:, None, None, :, None],
        w_first.reshape(blocks, block, groups, 1, inner),
        jnp.zeros((), BF16),
    ).reshape(width, width)

    dense = 2 * rows * width * width
    back = call(back_kernel, shape((groups, rows, LANES), BF16), flops=dense, moved=1 << 21)(
        d_out, second
    )
    back = exchange(back, "ch")
    pair = call(pack_kernel, shape((devices, rows, LANES), BF16), flops=1 << 20, moved=1 << 21)(
        signal, filter_raw
    )
    pair = exchange(pair, "seq")
    grad_conv = call(
        grad_conv_kernel, shape((devices, rows // 2, LANES), BF16), flops=dense, moved=1 << 21
    )(back, first, gate)
    grad_conv = exchange(grad_conv, "seq")
    cost = dict(flops=10 * 10**9, moved=16 * 10**6)
    spec, conv = call(
        conv_kernel,
        (
            shape((classes, 2 * INNER, LANES), BF16),
            shape((devices, rows // 2, LANES), BF16),
        ),
        scratch,
        **cost,
    )(pair, forward, inverse)
    conv = exchange(conv, "seq")
    grads = call(adjoint_kernel, shape((devices, rows, LANES), BF16), scratch, **cost)(
        grad_conv, spec, forward, inverse
    )
    first_rows = blocks * (block // devices) * block // LANES
    mix, grad_gate, grad_first = call(
        mix_kernel,
        (
            shape((groups, rows, LANES), BF16),
            shape((rows, width), BF16),
            shape((devices, first_rows, LANES), F32),
        ),
        flops=3 * dense,
        moved=1 << 22,
    )(conv, back, first, gate)
    mix = exchange(mix, "ch")
    grads = exchange(grads, "seq")

    def second_body(mix_ref, d_out_ref, grad_first_ref, out_ref):
        second_kernel(mix_ref, d_out_ref, grad_first_ref, out_ref, inner, out_block)

    second_rows = inner * (across // devices) * out_block // LANES
    small = call(
        second_body,
        shape((devices, first_rows + second_rows, LANES), F32),
        flops=dense,
        moved=1 << 21,
    )(mix, d_out, grad_first)
    small = exchange(small, "seq").sum(axis=0)
    grad_first = (
        small[:first_rows]
        .reshape(blocks // 2, block // devices, 2, block)
        .transpose(2, 0, 1, 3)
        .reshape(blocks, block // devices, block)
    )
    grad_second = small[first_rows:].reshape(inner, across // devices, out_block)
    grad_signal, grad_filter = call(
        unpack_kernel,
        (shape((rows, width), BF16), shape((rows, width), BF16)),
        flops=1 << 20,
        moved=1 << 21,
    )(grads)
    return (grad_signal, grad_filter, grad_gate, grad_first, grad_second)


def shards(signal, filter_raw, gate, d_out, w_first, w_second):
    rows, width = signal.shape
    devices = lax.axis_size("seq")
    blocks, block, _ = w_first.shape
    inner, across, out_block = w_second.shape
    fits = (
        blocks == devices
        and block == HALF
        and width == devices * HALF
        and width == lax.axis_size("ch") * LANES
        and width == inner * out_block
        and blocks * inner == LANES
        and LANES // out_block == across // devices
        and lax.axis_size("ch") * inner == block
        and devices % lax.axis_size("ch") == 0
        and block // devices == 8
        and rows % (2 * INNER) == 0
        and (rows * devices // INNER) & (rows * devices // INNER - 1) == 0
    )
    body = shards_whole if fits else shards_general
    return body(signal, filter_raw, gate, d_out, w_first, w_second)


def solution(mesh):
    in_specs = (
        P("seq", "ch"),
        P("seq", "ch"),
        P("seq", "ch"),
        P("seq", "ch"),
        P("ch", None, None),
        P("ch", None, None),
    )
    out_specs = (
        P("seq", "ch"),
        P("seq", "ch"),
        P("seq", "ch"),
        P("ch", "seq", None),
        P("ch", "seq", None),
    )
    return jax.shard_map(shards, mesh=mesh, in_specs=in_specs, out_specs=out_specs, check_vma=False)
```

```python
import functools
import math

import jax
import jax.numpy as jnp
import ml_dtypes
import numpy as np
from jax import lax
from jax.experimental import pallas as pl
from jax.experimental.pallas import tpu as pltpu
from jax.sharding import PartitionSpec as P

HIGHEST = lax.Precision.HIGHEST


def counting(count):
    return jnp.arange(count, dtype=jnp.int32)


def phase_table(row_ids, col_ids, length, sign):
    angles = (
        2.0 * math.pi / length * (row_ids[:, None] * col_ids[None, :] % length).astype(jnp.float32)
    )
    return (jnp.cos(angles), sign * jnp.sin(angles))


def contract(form, table, real_part, imag_part):
    cosine, sine = table
    out_real = jnp.einsum(form, cosine, real_part, precision=HIGHEST) - jnp.einsum(
        form, sine, imag_part, precision=HIGHEST
    )
    out_imag = jnp.einsum(form, cosine, imag_part, precision=HIGHEST) + jnp.einsum(
        form, sine, real_part, precision=HIGHEST
    )
    return (out_real, out_imag)


def rotate(cosine, sine, real_part, imag_part):
    return (real_part * cosine - imag_part * sine, real_part * sine + imag_part * cosine)


def factors(length):
    return (length // 128, 128)


def local_forward(real_part, imag_part):
    fields, group, rows, width = real_part.shape
    outer, inner = factors(rows)
    real_part = real_part.reshape(fields, group, outer, inner, width)
    imag_part = imag_part.reshape(fields, group, outer, inner, width)
    real_part, imag_part = contract(
        "qa,fkabc->fkqbc",
        phase_table(counting(outer), counting(outer), outer, -1.0),
        real_part,
        imag_part,
    )
    cosine, sine = phase_table(counting(outer), counting(inner), rows, -1.0)
    real_part, imag_part = rotate(cosine[:, :, None], sine[:, :, None], real_part, imag_part)
    return contract(
        "rb,fkqbc->fkqrc",
        phase_table(counting(inner), counting(inner), inner, -1.0),
        real_part,
        imag_part,
    )


def local_inverse(real_part, imag_part):
    fields, group, outer, inner, width = real_part.shape
    rows = outer * inner
    real_part, imag_part = contract(
        "br,fkqrc->fkqbc",
        phase_table(counting(inner), counting(inner), inner, 1.0),
        real_part,
        imag_part,
    )
    cosine, sine = phase_table(counting(outer), counting(inner), rows, 1.0)
    real_part, imag_part = rotate(cosine[:, :, None], sine[:, :, None], real_part, imag_part)
    real_part, imag_part = contract(
        "aq,fkqbc->fkabc",
        phase_table(counting(outer), counting(outer), outer, 1.0),
        real_part,
        imag_part,
    )
    return (
        real_part.reshape(fields, group, rows, width),
        imag_part.reshape(fields, group, rows, width),
    )


def forward_transform(fields):
    devices = lax.axis_size("seq")
    count, rows, width = fields.shape
    piece = rows // devices
    span = 2 * devices
    whole = span * rows
    parts = lax.all_to_all(fields[:, None], "seq", split_axis=2, concat_axis=1, tiled=True)
    cosine, sine = phase_table(counting(span), counting(devices), span, -1.0)
    real_part = jnp.einsum("ka,fabc->fkbc", cosine, parts, precision=HIGHEST)
    imag_part = jnp.einsum("ka,fabc->fkbc", sine, parts, precision=HIGHEST)
    positions = lax.axis_index("seq") * piece + counting(piece)
    cosine, sine = phase_table(counting(span), positions, whole, -1.0)
    real_part, imag_part = rotate(cosine[:, :, None], sine[:, :, None], real_part, imag_part)
    spectrum = lax.all_to_all(
        jnp.stack([real_part, imag_part], axis=1), "seq", split_axis=2, concat_axis=3, tiled=True
    )
    return local_forward(spectrum[:, 0], spectrum[:, 1])


def inverse_transform(real_part, imag_part):
    devices = lax.axis_size("seq")
    real_part, imag_part = local_inverse(real_part, imag_part)
    group = real_part.shape[1]
    rows = real_part.shape[2]
    span = 2 * devices
    whole = span * rows
    classes = lax.axis_index("seq") * group + counting(group)
    cosine, sine = phase_table(classes, counting(rows), whole, 1.0)
    real_part, imag_part = rotate(cosine[:, :, None], sine[:, :, None], real_part, imag_part)
    gathered = lax.all_to_all(
        jnp.stack([real_part, imag_part], axis=1), "seq", split_axis=3, concat_axis=2, tiled=True
    )
    cosine, sine = phase_table(counting(devices), counting(span), span, 1.0)
    inverse_scale = 1.0 / whole
    out_real = (
        jnp.einsum("ak,fkbc->fabc", cosine, gathered[:, 0], precision=HIGHEST)
        - jnp.einsum("ak,fkbc->fabc", sine, gathered[:, 1], precision=HIGHEST)
    ) * inverse_scale
    slab = lax.all_to_all(out_real, "seq", split_axis=1, concat_axis=2, tiled=True)
    return slab[:, 0]


def adjoint_spectra(spectra_real, spectra_imag, incoming_real, incoming_imag):
    toward_signal_real = spectra_real[1] * incoming_real + spectra_imag[1] * incoming_imag
    toward_signal_imag = spectra_real[1] * incoming_imag - spectra_imag[1] * incoming_real
    toward_filter_real = spectra_real[0] * incoming_real + spectra_imag[0] * incoming_imag
    toward_filter_imag = spectra_real[0] * incoming_imag - spectra_imag[0] * incoming_real
    return (toward_signal_real, toward_signal_imag, toward_filter_real, toward_filter_imag)


def shards_general(signal, filter_raw, gate, d_out, w_first, w_second):
    rows, width = signal.shape
    scale = float(rows * lax.axis_size("seq")) ** (-0.5)
    signal_wide = signal.astype(jnp.float32)
    kernel = filter_raw.astype(jnp.float32) * scale
    spectra_real, spectra_imag = forward_transform(jnp.stack([signal_wide, kernel]))
    mixed_real = spectra_real[0] * spectra_real[1] - spectra_imag[0] * spectra_imag[1]
    mixed_imag = spectra_real[0] * spectra_imag[1] + spectra_imag[0] * spectra_real[1]
    conv = inverse_transform(mixed_real[None], mixed_imag[None])[0].astype(jnp.bfloat16)
    gate_wide = gate.astype(jnp.float32)
    product = (conv.astype(jnp.float32) * gate_wide).astype(jnp.bfloat16)
    blocks = w_first.shape[0]
    block = w_first.shape[1]
    product_blocks = product.reshape(rows, blocks, block)
    first_mix = jnp.einsum(
        "tij,ijk->tik", product_blocks, w_first, preferred_element_type=jnp.float32
    ).astype(jnp.bfloat16)
    received = lax.all_to_all(first_mix, "ch", split_axis=2, concat_axis=1, tiled=True)
    incoming = d_out.reshape(rows, w_second.shape[0], w_second.shape[1])
    second_back = jnp.einsum(
        "tko,kio->tki", incoming, w_second, preferred_element_type=jnp.float32
    ).astype(jnp.bfloat16)
    grad_second = jnp.einsum("tik,tko->kio", received, incoming, preferred_element_type=jnp.float32)
    returned = lax.all_to_all(second_back, "ch", split_axis=2, concat_axis=1, tiled=True)
    grad_product = jnp.einsum(
        "tki,ijk->tij", returned, w_first, preferred_element_type=jnp.float32
    ).reshape(rows, width)
    grad_first = jnp.einsum(
        "tij,tki->ijk", product_blocks, returned, preferred_element_type=jnp.float32
    )
    grad_gate = (grad_product * conv.astype(jnp.float32)).astype(jnp.bfloat16)
    grad_conv = grad_product * gate_wide
    incoming_real, incoming_imag = forward_transform(grad_conv[None])
    sig_real, sig_imag, fil_real, fil_imag = adjoint_spectra(
        spectra_real, spectra_imag, incoming_real[0], incoming_imag[0]
    )
    results = inverse_transform(jnp.stack([sig_real, fil_real]), jnp.stack([sig_imag, fil_imag]))
    grad_signal = results[0].astype(jnp.bfloat16)
    grad_filter = (results[1] * scale).astype(jnp.bfloat16)
    grad_first = lax.psum_scatter(
        grad_first.astype(jnp.bfloat16), "seq", scatter_dimension=1, tiled=True
    ).astype(jnp.float32)
    grad_second = lax.psum_scatter(grad_second, "seq", scatter_dimension=1, tiled=True)
    return (grad_signal, grad_filter, grad_gate, grad_first, grad_second)


F32 = jnp.float32
BF16 = jnp.bfloat16
LANES = 128
HALF = 64
INNER = 128
CHUNK = 16


def dft_tables(outer, scale):
    length = outer * INNER
    q = np.arange(outer // 2 + 1)[:, None, None]
    r = np.arange(INNER)[None, :, None]
    b = np.arange(INNER)[None, None, :]
    angle = 2.0 * np.pi / length * ((b * (q + outer * r)) % length)
    c, s = np.cos(angle), np.sin(angle)
    forward = np.concatenate(
        [np.concatenate([c, s], axis=2), np.concatenate([-s, c], axis=2)], axis=1
    )
    inverse = forward.transpose(0, 2, 1) * (scale / length)
    return forward.astype(ml_dtypes.bfloat16), inverse.astype(ml_dtypes.bfloat16)


def times(value, cosine, sine):
    real, imag = value
    if imag is None:
        return (real * cosine, real * sine)
    return (real * cosine - imag * sine, real * sine + imag * cosine)


def real_dft(values, length):
    if length == 2:
        return [(values[0], None), (values[0], None)]
    even = real_dft(values[0::2], length // 2)
    odd = real_dft(values[1::2], length // 2)
    half, quarter = length // 2, length // 4
    out = [None] * (half + 1)
    for q in range(quarter + 1):
        er, ei = even[q]
        if q == 0:
            out[0] = (er + odd[0][0], None)
            out[half] = (er - odd[0][0], None)
        elif q == quarter:
            out[q] = (er, -odd[q][0])
        else:
            angle = 2.0 * math.pi * q / length
            tr, ti = times(odd[q], math.cos(angle), -math.sin(angle))
            out[q] = (er + tr, ei + ti)
            out[half - q] = (er - tr, ti - ei)
    return out


def real_inverse(values, length):
    if length == 2:
        return [values[0][0] + values[1][0]]
    half, quarter = length // 2, length // 4
    even, odd = [], []
    for q in range(quarter + 1):
        zr, zi = values[q]
        if q == 0:
            wr = values[half][0]
            even.append((zr + wr, None))
            odd.append((zr - wr, None))
        elif q == quarter:
            even.append((zr + zr, None))
            odd.append((-(zi + zi), None))
        else:
            wr, wi = values[half - q]
            even.append((zr + wr, zi - wi))
            angle = 2.0 * math.pi * q / length
            odd.append(times((zr - wr, zi + wi), math.cos(angle), math.sin(angle)))
    out = [None] * half
    out[0::2] = real_inverse(even, half)
    out[1::2] = real_inverse(odd, half)
    return out


def low_lanes(rows):
    return lax.broadcasted_iota(jnp.int32, (rows, LANES), 1) < HALF


def swap(value):
    return pltpu.roll(value, HALF, 1)


def store_classes(y_ref, rows, spectrum):
    for q, (real, imag) in enumerate(spectrum):
        y_ref[q, pl.ds(rows, CHUNK), :] = real.astype(BF16)
        imag = jnp.zeros_like(real) if imag is None else imag
        y_ref[q, pl.ds(INNER + rows, CHUNK), :] = imag.astype(BF16)


def load_classes(z_ref, rows, classes):
    out = []
    for q in range(classes):
        real = z_ref[q, pl.ds(rows, CHUNK), :]
        edge = q == 0 or q == classes - 1
        out.append((real, None if edge else z_ref[q, pl.ds(INNER + rows, CHUNK), :]))
    return out


def pack_kernel(signal_ref, filter_ref, out_ref):
    rows = signal_ref.shape[0]
    low = low_lanes(rows)
    for p in range(out_ref.shape[0] // 2):
        cols = slice(p * LANES, (p + 1) * LANES)
        a = signal_ref[:, cols].astype(F32)
        b = filter_ref[:, cols].astype(F32)
        out_ref[2 * p] = jnp.where(low, a, swap(b)).astype(BF16)
        out_ref[2 * p + 1] = jnp.where(low, swap(a), b).astype(BF16)


def unpack_kernel(in_ref, signal_ref, filter_ref):
    rows = signal_ref.shape[0]
    low = low_lanes(rows)
    for p in range(in_ref.shape[0] // 2):
        cols = slice(p * LANES, (p + 1) * LANES)
        a = in_ref[2 * p].astype(F32)
        b = in_ref[2 * p + 1].astype(F32)
        filter_ref[:, cols] = jnp.where(low, a, swap(b)).astype(BF16)
        signal_ref[:, cols] = jnp.where(low, swap(a), b).astype(BF16)


def conv_kernel(pair_ref, forward_ref, inverse_ref, spec_ref, conv_ref, y_ref, z_ref):
    devices, rows, _ = pair_ref.shape
    classes = forward_ref.shape[0]
    outer = 2 * (classes - 1)
    tiles = rows // INNER

    def first(j, carry):
        at = pl.multiple_of(j * CHUNK, CHUNK)
        points = [
            pair_ref[a // tiles, pl.ds((a % tiles) * INNER + at, CHUNK), :].astype(F32)
            for a in range(outer // 2)
        ]
        store_classes(y_ref, at, real_dft(points, outer))
        return carry

    lax.fori_loop(0, INNER // CHUNK, first, 0)

    def middle(q, carry):
        x = jnp.dot(forward_ref[q], y_ref[q], preferred_element_type=F32)
        spec_ref[q] = x.astype(BF16)
        o = swap(x)
        xr, xi, orr, oi = x[:INNER], x[INNER:], o[:INNER], o[INNER:]
        mixed = jnp.concatenate([xr * orr - xi * oi, xr * oi + xi * orr], axis=0)
        z_ref[q] = jnp.dot(inverse_ref[q], mixed.astype(BF16), preferred_element_type=F32)
        return carry

    lax.fori_loop(0, classes, middle, 0, unroll=3)
    low = low_lanes(CHUNK)
    halves = tiles // 2

    def last(j, carry):
        at = pl.multiple_of(j * CHUNK, CHUNK)
        points = real_inverse(load_classes(z_ref, at, classes), outer)
        for s in range(devices):
            for m in range(halves):
                a = s * tiles + m
                value = jnp.where(low, points[a], points[a + halves])
                conv_ref[s, pl.ds(m * INNER + at, CHUNK), :] = value.astype(BF16)
        return carry

    lax.fori_loop(0, INNER // CHUNK, last, 0)


def adjoint_kernel(grad_ref, spec_ref, forward_ref, inverse_ref, out_ref, y_ref, z_ref):
    devices, packed, _ = grad_ref.shape
    classes = forward_ref.shape[0]
    outer = 2 * (classes - 1)
    halves = packed // INNER
    tiles = 2 * halves
    low = low_lanes(CHUNK)

    def first(j, carry):
        at = pl.multiple_of(j * CHUNK, CHUNK)
        points = [None] * (outer // 2)
        for s in range(devices):
            for m in range(halves):
                value = grad_ref[s, pl.ds(m * INNER + at, CHUNK), :].astype(F32)
                other = swap(value)
                points[s * tiles + m] = jnp.where(low, value, other)
                points[s * tiles + halves + m] = jnp.where(low, other, value)
        store_classes(y_ref, at, real_dft(points, outer))
        return carry

    lax.fori_loop(0, INNER // CHUNK, first, 0)

    def middle(q, carry):
        g = jnp.dot(forward_ref[q], y_ref[q], preferred_element_type=F32)
        x = spec_ref[q].astype(F32)
        gr, gi, xr, xi = g[:INNER], g[INNER:], x[:INNER], x[INNER:]
        mixed = jnp.concatenate([xr * gr + xi * gi, xr * gi - xi * gr], axis=0)
        z_ref[q] = jnp.dot(inverse_ref[q], mixed.astype(BF16), preferred_element_type=F32)
        return carry

    lax.fori_loop(0, classes, middle, 0, unroll=3)

    def last(j, carry):
        at = pl.multiple_of(j * CHUNK, CHUNK)
        points = real_inverse(load_classes(z_ref, at, classes), outer)
        for a in range(outer // 2):
            out_ref[a // tiles, pl.ds((a % tiles) * INNER + at, CHUNK), :] = points[a].astype(BF16)
        return carry

    lax.fori_loop(0, INNER // CHUNK, last, 0)


def joined(ref):
    return jnp.concatenate([ref[c] for c in range(ref.shape[0])], axis=1)


def grad_product_of(back, first):
    return lax.dot_general(back, first, (((1,), (1,)), ((), ())), preferred_element_type=F32)


def grad_conv_kernel(back_ref, first_ref, gate_ref, out_ref):
    value = grad_product_of(joined(back_ref), first_ref[...]) * gate_ref[...].astype(F32)
    half = value.shape[0] // 2
    low = low_lanes(half)
    for p in range(out_ref.shape[0] // 2):
        top = value[:half, p * LANES : (p + 1) * LANES]
        bottom = value[half:, p * LANES : (p + 1) * LANES]
        out_ref[2 * p] = jnp.where(low, top, swap(bottom)).astype(BF16)
        out_ref[2 * p + 1] = jnp.where(low, swap(top), bottom).astype(BF16)


def mix_kernel(conv_ref, back_ref, first_ref, gate_ref, mix_ref, grad_gate_ref, grad_first_ref):
    devices, half, _ = conv_ref.shape
    low = low_lanes(half)
    parts = []
    for p in range(devices // 2):
        a = conv_ref[2 * p].astype(F32)
        b = conv_ref[2 * p + 1].astype(F32)
        parts.append(
            jnp.concatenate([jnp.where(low, a, swap(b)), jnp.where(low, swap(a), b)], axis=0)
        )
    conv = jnp.concatenate(parts, axis=1)
    product = (conv * gate_ref[...].astype(F32)).astype(BF16)
    first = first_ref[...]
    mix = jnp.dot(product, first, preferred_element_type=F32).astype(BF16)
    groups = mix_ref.shape[0]
    for c in range(groups):
        mix_ref[c] = mix[:, c * LANES : (c + 1) * LANES]
    back = joined(back_ref)
    grad_gate_ref[...] = (grad_product_of(back, first) * conv).astype(BF16)
    whole = lax.dot_general(product, back, (((0,), (0,)), ((), ())), preferred_element_type=F32)
    count = whole.shape[0]
    lane = lax.broadcasted_iota(jnp.int32, (count, LANES), 1)
    row = lax.broadcasted_iota(jnp.int32, (count, LANES), 0)
    inner = LANES // devices
    keep = lane // inner == row // (count // devices)
    grads = jnp.zeros((count, LANES), F32)
    for c in range(groups):
        value = jnp.where(keep, whole[:, c * LANES : (c + 1) * LANES], 0.0)
        shift = inner
        while shift < LANES:
            value = value + pltpu.roll(value, shift, 1)
            shift *= 2
        grads = jnp.where((lane // inner) % groups == c, value, grads)
    block = count // devices
    piece = block // devices
    pairs = devices // 2
    small = low_lanes(piece)
    for i in range(pairs):
        for s in range(devices):
            a = grads[i * block + s * piece : i * block + (s + 1) * piece]
            k = i + pairs
            b = grads[k * block + s * piece : k * block + (s + 1) * piece]
            grad_first_ref[s, i * piece : (i + 1) * piece, :] = jnp.where(small, a, b)


def second_kernel(mix_ref, d_out_ref, grad_first_ref, out_ref, inner, width):
    groups = mix_ref.shape[0]
    devices, first_rows, _ = grad_first_ref.shape
    out_ref[:, :first_rows, :] = grad_first_ref[...]
    d_out = d_out_ref[...]
    lane = lax.broadcasted_iota(jnp.int32, (LANES, LANES), 1)
    row = lax.broadcasted_iota(jnp.int32, (LANES, LANES), 0)
    folds = LANES // width
    per = devices // groups
    slot = lax.broadcasted_iota(jnp.int32, (inner, LANES), 1) // width
    for c in range(groups):
        whole = lax.dot_general(
            mix_ref[c], d_out, (((0,), (0,)), ((), ())), preferred_element_type=F32
        )
        total = jnp.zeros((LANES, LANES), F32)
        for g in range(whole.shape[1] // LANES):
            keep = lane // width + g * folds == row % inner
            total = total + jnp.where(keep, whole[:, g * LANES : (g + 1) * LANES], 0.0)
        shift = width
        while shift < LANES:
            total = total + pltpu.roll(total, shift, 1)
            shift *= 2
        for d in range(per):
            base = d * folds * inner
            piece = jnp.zeros((inner, LANES), F32)
            for i in range(folds):
                piece = jnp.where(slot == i, total[base + i * inner : base + (i + 1) * inner], piece)
            out_ref[c * per + d, first_rows:, :] = piece


PAIR, BACK, GRAD, CONV, RESULT, MIX, SMALL = range(7)


class Exchange:
    def __init__(self, number, axis, count, send, recv, send_sem, recv_sem):
        self.axis, self.count, self.send, self.recv = axis, count, send, recv
        self.number, self.send_sem, self.recv_sem = number, send_sem, recv_sem
        self.me = lax.axis_index(axis)

    def copy(self, peer, slot):
        return pltpu.make_async_remote_copy(
            src_ref=self.send.at[peer],
            dst_ref=self.recv.at[slot],
            send_sem=self.send_sem.at[self.number, peer],
            recv_sem=self.recv_sem.at[self.number, slot],
            device_id={self.axis: peer},
            device_id_type=pl.DeviceIdType.MESH,
        )

    def peers(self):
        return [lax.rem(self.me + d, self.count) for d in range(1, self.count)]

    def start(self):
        for peer in self.peers():
            self.copy(peer, self.me).start()
        self.recv[self.me] = self.send[self.me]

    def wait_recv(self):
        for peer in self.peers():
            self.copy(peer, peer).wait_recv()

    def wait_send(self):
        for peer in self.peers():
            self.copy(peer, self.me).wait_send()


def spread(values, pick):
    return jnp.dot(values, pick.astype(F32).astype(BF16), preferred_element_type=F32)


def first_matrix(w_ref, blocks, inner):
    rows, block = w_ref.shape
    shape = (block, rows)
    k = lax.broadcasted_iota(jnp.int32, shape, 0)
    col = lax.broadcasted_iota(jnp.int32, shape, 1)
    wide = spread(w_ref[...], k == (col // LANES) * inner + col % inner)
    row = lax.broadcasted_iota(jnp.int32, wide.shape, 0)
    col = lax.broadcasted_iota(jnp.int32, wide.shape, 1)
    return jnp.where(row // block == (col % LANES) // inner, wide, 0.0).astype(BF16)


def second_matrix(w_ref, inner):
    rows, width = w_ref.shape
    across = rows // inner
    r = lax.broadcasted_iota(jnp.int32, (rows, rows), 0)
    c = lax.broadcasted_iota(jnp.int32, (rows, rows), 1)
    order = (c == (r % inner) * across + r // inner).astype(F32).astype(BF16)
    turned = jnp.dot(order, w_ref[...], preferred_element_type=F32).astype(BF16)
    o = lax.broadcasted_iota(jnp.int32, (width, inner * width), 0)
    c = lax.broadcasted_iota(jnp.int32, (width, inner * width), 1)
    wide = spread(turned, o == c % width)
    row = lax.broadcasted_iota(jnp.int32, wide.shape, 0)
    col = lax.broadcasted_iota(jnp.int32, wide.shape, 1)
    return jnp.where(row % inner == col // width, wide, 0.0).astype(BF16)


def whole_kernel(
    devices,
    groups,
    blocks,
    inner,
    out_block,
    signal_ref,
    filter_ref,
    gate_ref,
    d_out_ref,
    w_first_ref,
    w_second_ref,
    forward_hbm,
    inverse_hbm,
    grad_signal_ref,
    grad_filter_ref,
    grad_gate_ref,
    small_ref,
    *scratch,
):
    buffers, rest = scratch[:14], scratch[14:]
    (forward, inverse, spec, y_ref, z_ref, first, grad_first) = rest[:7]
    table_sem, send_sem, recv_sem = rest[7:]
    axes = ["seq", "ch", "seq", "seq", "seq", "ch", "seq"]
    counts = {"seq": devices, "ch": groups}
    exchanges = [
        Exchange(n, axis, counts[axis], buffers[2 * n], buffers[2 * n + 1], send_sem, recv_sem)
        for n, axis in enumerate(axes)
    ]
    tables = [
        pltpu.make_async_copy(forward_hbm, forward, table_sem.at[0]),
        pltpu.make_async_copy(inverse_hbm, inverse, table_sem.at[1]),
    ]
    barrier = pltpu.get_barrier_semaphore()
    for exchange in (exchanges[PAIR], exchanges[BACK]):
        for peer in exchange.peers():
            pl.semaphore_signal(
                barrier,
                inc=1,
                device_id={exchange.axis: peer},
                device_id_type=pl.DeviceIdType.MESH,
            )
    for table in tables:
        table.start()
    pack_kernel(signal_ref, filter_ref, exchanges[PAIR].send)
    pl.semaphore_wait(barrier, devices + groups - 2)
    exchanges[PAIR].start()

    second = second_matrix(w_second_ref, inner)
    back = lax.dot_general(
        d_out_ref[...], second, (((1,), (1,)), ((), ())), preferred_element_type=F32
    ).astype(BF16)
    for c in range(groups):
        exchanges[BACK].send[c] = back[:, c * LANES : (c + 1) * LANES]
    exchanges[BACK].start()
    first[...] = first_matrix(w_first_ref, blocks, inner)
    exchanges[BACK].wait_recv()
    back_ref = exchanges[BACK].recv
    grad_conv_kernel(back_ref, first, gate_ref, exchanges[GRAD].send)
    exchanges[GRAD].start()
    for table in tables:
        table.wait()
    exchanges[PAIR].wait_recv()
    conv_kernel(
        exchanges[PAIR].recv, forward, inverse, spec, exchanges[CONV].send, y_ref, z_ref
    )
    exchanges[CONV].start()
    exchanges[GRAD].wait_recv()
    adjoint_kernel(
        exchanges[GRAD].recv, spec, forward, inverse, exchanges[RESULT].send, y_ref, z_ref
    )
    exchanges[RESULT].start()
    exchanges[CONV].wait_recv()
    mix_kernel(
        exchanges[CONV].recv,
        back_ref,
        first,
        gate_ref,
        exchanges[MIX].send,
        grad_gate_ref,
        grad_first,
    )
    exchanges[MIX].start()
    exchanges[MIX].wait_recv()
    second_kernel(
        exchanges[MIX].recv, d_out_ref, grad_first, exchanges[SMALL].send, inner, out_block
    )
    exchanges[SMALL].start()
    exchanges[RESULT].wait_recv()
    unpack_kernel(exchanges[RESULT].recv, grad_signal_ref, grad_filter_ref)
    exchanges[SMALL].wait_recv()
    total = exchanges[SMALL].recv[0]
    for s in range(1, devices):
        total = total + exchanges[SMALL].recv[s]
    small_ref[...] = total
    for exchange in exchanges:
        exchange.wait_send()


def shards_whole(signal, filter_raw, gate, d_out, w_first, w_second):
    rows, width = signal.shape
    devices = lax.axis_size("seq")
    groups = lax.axis_size("ch")
    length = rows * devices
    outer = 2 * length // INNER
    classes = outer // 2 + 1
    forward, inverse = (jnp.asarray(t) for t in dft_tables(outer, float(length) ** (-0.5)))
    blocks, block, _ = w_first.shape
    inner, across, out_block = w_second.shape
    first_rows = blocks * (block // devices) * block // LANES
    second_rows = inner * (across // devices) * out_block // LANES
    small_rows = first_rows + second_rows
    wide = ((devices, rows, LANES), BF16)
    half = ((devices, rows // 2, LANES), BF16)
    mixed = ((groups, rows, LANES), BF16)
    small = ((devices, small_rows, LANES), F32)
    buffers = [
        pltpu.VMEM(*kind)
        for kind in (wide, mixed, half, half, wide, mixed, small)
        for _ in range(2)
    ]
    vmem = pl.BlockSpec(memory_space=pltpu.VMEM)
    anywhere = pl.BlockSpec(memory_space=pl.ANY)
    field = jax.ShapeDtypeStruct((rows, width), BF16)
    grad_signal, grad_filter, grad_gate, sums = pl.pallas_call(
        functools.partial(whole_kernel, devices, groups, blocks, inner, out_block),
        out_shape=(field, field, field, jax.ShapeDtypeStruct((small_rows, LANES), F32)),
        in_specs=[vmem] * 6 + [anywhere] * 2,
        out_specs=(vmem,) * 4,
        scratch_shapes=buffers
        + [
            pltpu.VMEM(forward.shape, BF16),
            pltpu.VMEM(inverse.shape, BF16),
            pltpu.VMEM((classes, 2 * INNER, LANES), BF16),
            pltpu.VMEM((classes, 2 * INNER, LANES), BF16),
            pltpu.VMEM((classes, 2 * INNER, LANES), F32),
            pltpu.VMEM((width, width), BF16),
            pltpu.VMEM((devices, first_rows, LANES), F32),
            pltpu.SemaphoreType.DMA((2,)),
            pltpu.SemaphoreType.DMA((7, devices)),
            pltpu.SemaphoreType.DMA((7, devices)),
        ],
        compiler_params=pltpu.CompilerParams(
            collective_id=0, has_side_effects=True, vmem_limit_bytes=50 * 1024 * 1024
        ),
        cost_estimate=pl.CostEstimate(
            flops=20 * 10**9, bytes_accessed=16 * 10**6, transcendentals=0
        ),
    )(
        signal,
        filter_raw,
        gate,
        d_out,
        w_first.reshape(blocks * block, block),
        w_second.reshape(inner * across, out_block),
        forward,
        inverse,
    )
    grad_first = (
        sums[:first_rows]
        .reshape(blocks // 2, block // devices, 2, block)
        .transpose(2, 0, 1, 3)
        .reshape(blocks, block // devices, block)
    )
    grad_second = sums[first_rows:].reshape(inner, across // devices, out_block)
    return (grad_signal, grad_filter, grad_gate, grad_first, grad_second)


def shards(signal, filter_raw, gate, d_out, w_first, w_second):
    rows, width = signal.shape
    devices = lax.axis_size("seq")
    blocks, block, _ = w_first.shape
    inner, across, out_block = w_second.shape
    fits = (
        blocks == devices
        and block == HALF
        and width == devices * HALF
        and width == lax.axis_size("ch") * LANES
        and width == inner * out_block
        and blocks * inner == LANES
        and LANES // out_block == across // devices
        and lax.axis_size("ch") * inner == block
        and devices % lax.axis_size("ch") == 0
        and block // devices == 8
        and rows % (2 * INNER) == 0
        and (rows * devices // INNER) & (rows * devices // INNER - 1) == 0
    )
    body = shards_whole if fits else shards_general
    return body(signal, filter_raw, gate, d_out, w_first, w_second)


def solution(mesh):
    in_specs = (
        P("seq", "ch"),
        P("seq", "ch"),
        P("seq", "ch"),
        P("seq", "ch"),
        P("ch", None, None),
        P("ch", None, None),
    )
    out_specs = (
        P("seq", "ch"),
        P("seq", "ch"),
        P("seq", "ch"),
        P("ch", "seq", None),
        P("ch", "seq", None),
    )
    return jax.shard_map(shards, mesh=mesh, in_specs=in_specs, out_specs=out_specs, check_vma=False)
```

```python
import functools
import math

import jax
import jax.numpy as jnp
import ml_dtypes
import numpy as np
from jax import lax
from jax.experimental import pallas as pl
from jax.experimental.pallas import tpu as pltpu
from jax.sharding import PartitionSpec as P

HIGHEST = lax.Precision.HIGHEST


def counting(count):
    return jnp.arange(count, dtype=jnp.int32)


def phase_table(row_ids, col_ids, length, sign):
    angles = (
        2.0 * math.pi / length * (row_ids[:, None] * col_ids[None, :] % length).astype(jnp.float32)
    )
    return (jnp.cos(angles), sign * jnp.sin(angles))


def contract(form, table, real_part, imag_part):
    cosine, sine = table
    out_real = jnp.einsum(form, cosine, real_part, precision=HIGHEST) - jnp.einsum(
        form, sine, imag_part, precision=HIGHEST
    )
    out_imag = jnp.einsum(form, cosine, imag_part, precision=HIGHEST) + jnp.einsum(
        form, sine, real_part, precision=HIGHEST
    )
    return (out_real, out_imag)


def rotate(cosine, sine, real_part, imag_part):
    return (real_part * cosine - imag_part * sine, real_part * sine + imag_part * cosine)


def factors(length):
    return (length // 128, 128)


def local_forward(real_part, imag_part):
    fields, group, rows, width = real_part.shape
    outer, inner = factors(rows)
    real_part = real_part.reshape(fields, group, outer, inner, width)
    imag_part = imag_part.reshape(fields, group, outer, inner, width)
    real_part, imag_part = contract(
        "qa,fkabc->fkqbc",
        phase_table(counting(outer), counting(outer), outer, -1.0),
        real_part,
        imag_part,
    )
    cosine, sine = phase_table(counting(outer), counting(inner), rows, -1.0)
    real_part, imag_part = rotate(cosine[:, :, None], sine[:, :, None], real_part, imag_part)
    return contract(
        "rb,fkqbc->fkqrc",
        phase_table(counting(inner), counting(inner), inner, -1.0),
        real_part,
        imag_part,
    )


def local_inverse(real_part, imag_part):
    fields, group, outer, inner, width = real_part.shape
    rows = outer * inner
    real_part, imag_part = contract(
        "br,fkqrc->fkqbc",
        phase_table(counting(inner), counting(inner), inner, 1.0),
        real_part,
        imag_part,
    )
    cosine, sine = phase_table(counting(outer), counting(inner), rows, 1.0)
    real_part, imag_part = rotate(cosine[:, :, None], sine[:, :, None], real_part, imag_part)
    real_part, imag_part = contract(
        "aq,fkqbc->fkabc",
        phase_table(counting(outer), counting(outer), outer, 1.0),
        real_part,
        imag_part,
    )
    return (
        real_part.reshape(fields, group, rows, width),
        imag_part.reshape(fields, group, rows, width),
    )


def forward_transform(fields):
    devices = lax.axis_size("seq")
    count, rows, width = fields.shape
    piece = rows // devices
    span = 2 * devices
    whole = span * rows
    parts = lax.all_to_all(fields[:, None], "seq", split_axis=2, concat_axis=1, tiled=True)
    cosine, sine = phase_table(counting(span), counting(devices), span, -1.0)
    real_part = jnp.einsum("ka,fabc->fkbc", cosine, parts, precision=HIGHEST)
    imag_part = jnp.einsum("ka,fabc->fkbc", sine, parts, precision=HIGHEST)
    positions = lax.axis_index("seq") * piece + counting(piece)
    cosine, sine = phase_table(counting(span), positions, whole, -1.0)
    real_part, imag_part = rotate(cosine[:, :, None], sine[:, :, None], real_part, imag_part)
    spectrum = lax.all_to_all(
        jnp.stack([real_part, imag_part], axis=1), "seq", split_axis=2, concat_axis=3, tiled=True
    )
    return local_forward(spectrum[:, 0], spectrum[:, 1])


def inverse_transform(real_part, imag_part):
    devices = lax.axis_size("seq")
    real_part, imag_part = local_inverse(real_part, imag_part)
    group = real_part.shape[1]
    rows = real_part.shape[2]
    span = 2 * devices
    whole = span * rows
    classes = lax.axis_index("seq") * group + counting(group)
    cosine, sine = phase_table(classes, counting(rows), whole, 1.0)
    real_part, imag_part = rotate(cosine[:, :, None], sine[:, :, None], real_part, imag_part)
    gathered = lax.all_to_all(
        jnp.stack([real_part, imag_part], axis=1), "seq", split_axis=3, concat_axis=2, tiled=True
    )
    cosine, sine = phase_table(counting(devices), counting(span), span, 1.0)
    inverse_scale = 1.0 / whole
    out_real = (
        jnp.einsum("ak,fkbc->fabc", cosine, gathered[:, 0], precision=HIGHEST)
        - jnp.einsum("ak,fkbc->fabc", sine, gathered[:, 1], precision=HIGHEST)
    ) * inverse_scale
    slab = lax.all_to_all(out_real, "seq", split_axis=1, concat_axis=2, tiled=True)
    return slab[:, 0]


def adjoint_spectra(spectra_real, spectra_imag, incoming_real, incoming_imag):
    toward_signal_real = spectra_real[1] * incoming_real + spectra_imag[1] * incoming_imag
    toward_signal_imag = spectra_real[1] * incoming_imag - spectra_imag[1] * incoming_real
    toward_filter_real = spectra_real[0] * incoming_real + spectra_imag[0] * incoming_imag
    toward_filter_imag = spectra_real[0] * incoming_imag - spectra_imag[0] * incoming_real
    return (toward_signal_real, toward_signal_imag, toward_filter_real, toward_filter_imag)


def shards_general(signal, filter_raw, gate, d_out, w_first, w_second):
    rows, width = signal.shape
    scale = float(rows * lax.axis_size("seq")) ** (-0.5)
    signal_wide = signal.astype(jnp.float32)
    kernel = filter_raw.astype(jnp.float32) * scale
    spectra_real, spectra_imag = forward_transform(jnp.stack([signal_wide, kernel]))
    mixed_real = spectra_real[0] * spectra_real[1] - spectra_imag[0] * spectra_imag[1]
    mixed_imag = spectra_real[0] * spectra_imag[1] + spectra_imag[0] * spectra_real[1]
    conv = inverse_transform(mixed_real[None], mixed_imag[None])[0].astype(jnp.bfloat16)
    gate_wide = gate.astype(jnp.float32)
    product = (conv.astype(jnp.float32) * gate_wide).astype(jnp.bfloat16)
    blocks = w_first.shape[0]
    block = w_first.shape[1]
    product_blocks = product.reshape(rows, blocks, block)
    first_mix = jnp.einsum(
        "tij,ijk->tik", product_blocks, w_first, preferred_element_type=jnp.float32
    ).astype(jnp.bfloat16)
    received = lax.all_to_all(first_mix, "ch", split_axis=2, concat_axis=1, tiled=True)
    incoming = d_out.reshape(rows, w_second.shape[0], w_second.shape[1])
    second_back = jnp.einsum(
        "tko,kio->tki", incoming, w_second, preferred_element_type=jnp.float32
    ).astype(jnp.bfloat16)
    grad_second = jnp.einsum("tik,tko->kio", received, incoming, preferred_element_type=jnp.float32)
    returned = lax.all_to_all(second_back, "ch", split_axis=2, concat_axis=1, tiled=True)
    grad_product = jnp.einsum(
        "tki,ijk->tij", returned, w_first, preferred_element_type=jnp.float32
    ).reshape(rows, width)
    grad_first = jnp.einsum(
        "tij,tki->ijk", product_blocks, returned, preferred_element_type=jnp.float32
    )
    grad_gate = (grad_product * conv.astype(jnp.float32)).astype(jnp.bfloat16)
    grad_conv = grad_product * gate_wide
    incoming_real, incoming_imag = forward_transform(grad_conv[None])
    sig_real, sig_imag, fil_real, fil_imag = adjoint_spectra(
        spectra_real, spectra_imag, incoming_real[0], incoming_imag[0]
    )
    results = inverse_transform(jnp.stack([sig_real, fil_real]), jnp.stack([sig_imag, fil_imag]))
    grad_signal = results[0].astype(jnp.bfloat16)
    grad_filter = (results[1] * scale).astype(jnp.bfloat16)
    grad_first = lax.psum_scatter(
        grad_first.astype(jnp.bfloat16), "seq", scatter_dimension=1, tiled=True
    ).astype(jnp.float32)
    grad_second = lax.psum_scatter(grad_second, "seq", scatter_dimension=1, tiled=True)
    return (grad_signal, grad_filter, grad_gate, grad_first, grad_second)


F32 = jnp.float32
BF16 = jnp.bfloat16
LANES = 128
HALF = 64
INNER = 128
CHUNK = 16
PARTS = 2


def dft_tables(outer, scale):
    length = outer * INNER
    q = np.arange(outer // 2 + 1)[:, None, None]
    r = np.arange(INNER)[None, :, None]
    b = np.arange(INNER)[None, None, :]
    angle = 2.0 * np.pi / length * ((b * (q + outer * r)) % length)
    c, s = np.cos(angle), np.sin(angle)
    forward = np.concatenate(
        [np.concatenate([c, s], axis=2), np.concatenate([-s, c], axis=2)], axis=1
    )
    inverse = forward.transpose(0, 2, 1) * (scale / length)
    return forward.astype(ml_dtypes.bfloat16), inverse.astype(ml_dtypes.bfloat16)


def times(value, cosine, sine):
    real, imag = value
    if imag is None:
        return (real * cosine, real * sine)
    return (real * cosine - imag * sine, real * sine + imag * cosine)


def real_dft(values, length):
    if length == 2:
        return [(values[0], None), (values[0], None)]
    even = real_dft(values[0::2], length // 2)
    odd = real_dft(values[1::2], length // 2)
    half, quarter = length // 2, length // 4
    out = [None] * (half + 1)
    for q in range(quarter + 1):
        er, ei = even[q]
        if q == 0:
            out[0] = (er + odd[0][0], None)
            out[half] = (er - odd[0][0], None)
        elif q == quarter:
            out[q] = (er, -odd[q][0])
        else:
            angle = 2.0 * math.pi * q / length
            tr, ti = times(odd[q], math.cos(angle), -math.sin(angle))
            out[q] = (er + tr, ei + ti)
            out[half - q] = (er - tr, ti - ei)
    return out


def real_inverse(values, length):
    if length == 2:
        return [values[0][0] + values[1][0]]
    half, quarter = length // 2, length // 4
    even, odd = [], []
    for q in range(quarter + 1):
        zr, zi = values[q]
        if q == 0:
            wr = values[half][0]
            even.append((zr + wr, None))
            odd.append((zr - wr, None))
        elif q == quarter:
            even.append((zr + zr, None))
            odd.append((-(zi + zi), None))
        else:
            wr, wi = values[half - q]
            even.append((zr + wr, zi - wi))
            angle = 2.0 * math.pi * q / length
            odd.append(times((zr - wr, zi + wi), math.cos(angle), math.sin(angle)))
    out = [None] * half
    out[0::2] = real_inverse(even, half)
    out[1::2] = real_inverse(odd, half)
    return out


def low_lanes(rows):
    return lax.broadcasted_iota(jnp.int32, (rows, LANES), 1) < HALF


def swap(value):
    return pltpu.roll(value, HALF, 1)


def store_classes(y_ref, rows, spectrum):
    for q, (real, imag) in enumerate(spectrum):
        y_ref[q, pl.ds(rows, CHUNK), :] = real.astype(BF16)
        imag = jnp.zeros_like(real) if imag is None else imag
        y_ref[q, pl.ds(INNER + rows, CHUNK), :] = imag.astype(BF16)


def load_classes(z_ref, rows, classes):
    out = []
    for q in range(classes):
        real = z_ref[q, pl.ds(rows, CHUNK), :]
        edge = q == 0 or q == classes - 1
        out.append((real, None if edge else z_ref[q, pl.ds(INNER + rows, CHUNK), :]))
    return out


def pack_part(signal_ref, filter_ref, out_ref, part):
    size = INNER // PARTS
    low = low_lanes(size)
    for p in range(out_ref.shape[0] // 2):
        cols = slice(p * LANES, (p + 1) * LANES)
        for m in range(signal_ref.shape[0] // INNER):
            source = slice(m * INNER + part * size, m * INNER + (part + 1) * size)
            rows = slice(m * size, (m + 1) * size)
            a = signal_ref[source, cols].astype(F32)
            b = filter_ref[source, cols].astype(F32)
            out_ref[2 * p, rows, :] = jnp.where(low, a, swap(b)).astype(BF16)
            out_ref[2 * p + 1, rows, :] = jnp.where(low, swap(a), b).astype(BF16)


def unpack_part(in_ref, signal_ref, filter_ref, part):
    size = INNER // PARTS
    low = low_lanes(size)
    for p in range(in_ref.shape[0] // 2):
        cols = slice(p * LANES, (p + 1) * LANES)
        for m in range(signal_ref.shape[0] // INNER):
            target = slice(m * INNER + part * size, m * INNER + (part + 1) * size)
            rows = slice(m * size, (m + 1) * size)
            a = in_ref[2 * p, rows, :].astype(F32)
            b = in_ref[2 * p + 1, rows, :].astype(F32)
            filter_ref[target, cols] = jnp.where(low, a, swap(b)).astype(BF16)
            signal_ref[target, cols] = jnp.where(low, swap(a), b).astype(BF16)


def conv_first(pair_ref, y_ref, part, outer):
    size = INNER // PARTS
    tiles = outer // 2 // pair_ref.shape[0]

    def first(j, carry):
        at = pl.multiple_of(j * CHUNK, CHUNK)
        points = [
            pair_ref[a // tiles, pl.ds((a % tiles) * size + at, CHUNK), :].astype(F32)
            for a in range(outer // 2)
        ]
        store_classes(y_ref, part * size + at, real_dft(points, outer))
        return carry

    lax.fori_loop(0, size // CHUNK, first, 0)


def conv_kernel(forward_ref, inverse_ref, spec_ref, conv_ref, y_ref, z_ref):
    devices, packed, _ = conv_ref.shape
    classes = forward_ref.shape[0]
    outer = 2 * (classes - 1)
    tiles = 2 * packed // INNER

    def middle(q, carry):
        x = jnp.dot(forward_ref[q], y_ref[q], preferred_element_type=F32)
        spec_ref[q] = x.astype(BF16)
        o = swap(x)
        xr, xi, orr, oi = x[:INNER], x[INNER:], o[:INNER], o[INNER:]
        mixed = jnp.concatenate([xr * orr - xi * oi, xr * oi + xi * orr], axis=0)
        z_ref[q] = jnp.dot(inverse_ref[q], mixed.astype(BF16), preferred_element_type=F32)
        return carry

    lax.fori_loop(0, classes, middle, 0, unroll=3)
    low = low_lanes(CHUNK)
    halves = tiles // 2

    def last(j, carry):
        at = pl.multiple_of(j * CHUNK, CHUNK)
        points = real_inverse(load_classes(z_ref, at, classes), outer)
        for s in range(devices):
            for m in range(halves):
                a = s * tiles + m
                value = jnp.where(low, points[a], points[a + halves])
                conv_ref[s, pl.ds(m * INNER + at, CHUNK), :] = value.astype(BF16)
        return carry

    lax.fori_loop(0, INNER // CHUNK, last, 0)


def adjoint_kernel(grad_ref, spec_ref, forward_ref, inverse_ref, y_ref, z_ref):
    devices, packed, _ = grad_ref.shape
    classes = forward_ref.shape[0]
    outer = 2 * (classes - 1)
    halves = packed // INNER
    tiles = 2 * halves
    low = low_lanes(CHUNK)

    def first(j, carry):
        at = pl.multiple_of(j * CHUNK, CHUNK)
        points = [None] * (outer // 2)
        for s in range(devices):
            for m in range(halves):
                value = grad_ref[s, pl.ds(m * INNER + at, CHUNK), :].astype(F32)
                other = swap(value)
                points[s * tiles + m] = jnp.where(low, value, other)
                points[s * tiles + halves + m] = jnp.where(low, other, value)
        store_classes(y_ref, at, real_dft(points, outer))
        return carry

    lax.fori_loop(0, INNER // CHUNK, first, 0)

    def middle(q, carry):
        g = jnp.dot(forward_ref[q], y_ref[q], preferred_element_type=F32)
        x = spec_ref[q].astype(F32)
        gr, gi, xr, xi = g[:INNER], g[INNER:], x[:INNER], x[INNER:]
        mixed = jnp.concatenate([xr * gr + xi * gi, xr * gi - xi * gr], axis=0)
        z_ref[q] = jnp.dot(inverse_ref[q], mixed.astype(BF16), preferred_element_type=F32)
        return carry

    lax.fori_loop(0, classes, middle, 0, unroll=3)


def adjoint_last(z_ref, out_ref, part):
    size = INNER // PARTS
    classes = z_ref.shape[0]
    outer = 2 * (classes - 1)
    tiles = outer // 2 // out_ref.shape[0]

    def last(j, carry):
        at = pl.multiple_of(j * CHUNK, CHUNK)
        points = real_inverse(load_classes(z_ref, part * size + at, classes), outer)
        for a in range(outer // 2):
            rows = pl.ds((a % tiles) * size + at, CHUNK)
            out_ref[a // tiles, rows, :] = points[a].astype(BF16)
        return carry

    lax.fori_loop(0, size // CHUNK, last, 0)


def joined(ref):
    return jnp.concatenate([ref[c] for c in range(ref.shape[0])], axis=1)


def grad_product_of(back, first):
    return lax.dot_general(back, first, (((1,), (1,)), ((), ())), preferred_element_type=F32)


def grad_conv_kernel(back_ref, first_ref, gate_ref, out_ref):
    value = grad_product_of(joined(back_ref), first_ref[...]) * gate_ref[...].astype(F32)
    half = value.shape[0] // 2
    low = low_lanes(half)
    for p in range(out_ref.shape[0] // 2):
        top = value[:half, p * LANES : (p + 1) * LANES]
        bottom = value[half:, p * LANES : (p + 1) * LANES]
        out_ref[2 * p] = jnp.where(low, top, swap(bottom)).astype(BF16)
        out_ref[2 * p + 1] = jnp.where(low, swap(top), bottom).astype(BF16)


def mix_kernel(conv_ref, back_ref, first_ref, gate_ref, mix_ref, grad_gate_ref, grad_first_ref):
    devices, half, _ = conv_ref.shape
    low = low_lanes(half)
    parts = []
    for p in range(devices // 2):
        a = conv_ref[2 * p].astype(F32)
        b = conv_ref[2 * p + 1].astype(F32)
        parts.append(
            jnp.concatenate([jnp.where(low, a, swap(b)), jnp.where(low, swap(a), b)], axis=0)
        )
    conv = jnp.concatenate(parts, axis=1)
    product = (conv * gate_ref[...].astype(F32)).astype(BF16)
    first = first_ref[...]
    mix = jnp.dot(product, first, preferred_element_type=F32).astype(BF16)
    groups = mix_ref.shape[0]
    for c in range(groups):
        mix_ref[c] = mix[:, c * LANES : (c + 1) * LANES]
    back = joined(back_ref)
    grad_gate_ref[...] = (grad_product_of(back, first) * conv).astype(BF16)
    whole = lax.dot_general(product, back, (((0,), (0,)), ((), ())), preferred_element_type=F32)
    count = whole.shape[0]
    lane = lax.broadcasted_iota(jnp.int32, (count, LANES), 1)
    row = lax.broadcasted_iota(jnp.int32, (count, LANES), 0)
    inner = LANES // devices
    keep = lane // inner == row // (count // devices)
    grads = jnp.zeros((count, LANES), F32)
    for c in range(groups):
        value = jnp.where(keep, whole[:, c * LANES : (c + 1) * LANES], 0.0)
        shift = inner
        while shift < LANES:
            value = value + pltpu.roll(value, shift, 1)
            shift *= 2
        grads = jnp.where((lane // inner) % groups == c, value, grads)
    block = count // devices
    piece = block // devices
    pairs = devices // 2
    small = low_lanes(piece)
    for i in range(pairs):
        for s in range(devices):
            a = grads[i * block + s * piece : i * block + (s + 1) * piece]
            k = i + pairs
            b = grads[k * block + s * piece : k * block + (s + 1) * piece]
            grad_first_ref[s, i * piece : (i + 1) * piece, :] = jnp.where(small, a, b)


def second_kernel(mix_ref, d_out_ref, grad_first_ref, out_ref, inner, width):
    groups = mix_ref.shape[0]
    devices, first_rows, _ = grad_first_ref.shape
    out_ref[:, :first_rows, :] = grad_first_ref[...]
    d_out = d_out_ref[...]
    lane = lax.broadcasted_iota(jnp.int32, (LANES, LANES), 1)
    row = lax.broadcasted_iota(jnp.int32, (LANES, LANES), 0)
    folds = LANES // width
    per = devices // groups
    slot = lax.broadcasted_iota(jnp.int32, (inner, LANES), 1) // width
    for c in range(groups):
        whole = lax.dot_general(
            mix_ref[c], d_out, (((0,), (0,)), ((), ())), preferred_element_type=F32
        )
        total = jnp.zeros((LANES, LANES), F32)
        for g in range(whole.shape[1] // LANES):
            keep = lane // width + g * folds == row % inner
            total = total + jnp.where(keep, whole[:, g * LANES : (g + 1) * LANES], 0.0)
        shift = width
        while shift < LANES:
            total = total + pltpu.roll(total, shift, 1)
            shift *= 2
        for d in range(per):
            base = d * folds * inner
            piece = jnp.zeros((inner, LANES), F32)
            for i in range(folds):
                piece = jnp.where(slot == i, total[base + i * inner : base + (i + 1) * inner], piece)
            out_ref[c * per + d, first_rows:, :] = piece


PAIR, BACK, GRAD, CONV, RESULT, MIX, SMALL = range(7)
INPUTS = 6


class Exchange:
    def __init__(self, number, axis, count, send, recv, send_sem, recv_sem):
        self.axis, self.count, self.send, self.recv = axis, count, send, recv
        self.number, self.send_sem, self.recv_sem = number, send_sem, recv_sem
        self.me = lax.axis_index(axis)

    def copy(self, peer, slot):
        return pltpu.make_async_remote_copy(
            src_ref=self.send.at[peer],
            dst_ref=self.recv.at[slot],
            send_sem=self.send_sem.at[self.number, peer],
            recv_sem=self.recv_sem.at[self.number, slot],
            device_id={self.axis: peer},
            device_id_type=pl.DeviceIdType.MESH,
        )

    def peers(self):
        return [lax.rem(self.me + d, self.count) for d in range(1, self.count)]

    def start(self):
        for peer in self.peers():
            self.copy(peer, self.me).start()
        self.recv[self.me] = self.send[self.me]

    def wait_recv(self):
        for peer in self.peers():
            self.copy(peer, peer).wait_recv()

    def wait_send(self):
        for peer in self.peers():
            self.copy(peer, self.me).wait_send()


def spread(values, pick):
    return jnp.dot(values, pick.astype(F32).astype(BF16), preferred_element_type=F32)


def first_matrix(w_ref, blocks, inner):
    rows, block = w_ref.shape
    shape = (block, rows)
    k = lax.broadcasted_iota(jnp.int32, shape, 0)
    col = lax.broadcasted_iota(jnp.int32, shape, 1)
    wide = spread(w_ref[...], k == (col // LANES) * inner + col % inner)
    row = lax.broadcasted_iota(jnp.int32, wide.shape, 0)
    col = lax.broadcasted_iota(jnp.int32, wide.shape, 1)
    return jnp.where(row // block == (col % LANES) // inner, wide, 0.0).astype(BF16)


def second_matrix(w_ref, inner):
    rows, width = w_ref.shape
    across = rows // inner
    r = lax.broadcasted_iota(jnp.int32, (rows, rows), 0)
    c = lax.broadcasted_iota(jnp.int32, (rows, rows), 1)
    order = (c == (r % inner) * across + r // inner).astype(F32).astype(BF16)
    turned = jnp.dot(order, w_ref[...], preferred_element_type=F32).astype(BF16)
    o = lax.broadcasted_iota(jnp.int32, (width, inner * width), 0)
    c = lax.broadcasted_iota(jnp.int32, (width, inner * width), 1)
    wide = spread(turned, o == c % width)
    row = lax.broadcasted_iota(jnp.int32, wide.shape, 0)
    col = lax.broadcasted_iota(jnp.int32, wide.shape, 1)
    return jnp.where(row % inner == col // width, wide, 0.0).astype(BF16)


def whole_kernel(
    devices,
    groups,
    blocks,
    inner,
    out_block,
    *refs,
):
    inputs, (forward_hbm, inverse_hbm) = refs[:INPUTS], refs[INPUTS : INPUTS + 2]
    refs = refs[INPUTS + 2 :]
    grad_signal_ref, grad_filter_ref, grad_gate_ref, small_ref = refs[:4]
    buffers, local, rest = refs[4:18], refs[18 : 18 + INPUTS], refs[18 + INPUTS :]
    (forward, inverse, spec, y_ref, z_ref, first, grad_first) = rest[:7]
    input_sem, send_sem, recv_sem = rest[7:]
    signal_ref, filter_ref, gate_ref, d_out_ref, w_first_ref, w_second_ref = local
    axes = ["seq", "ch", "seq", "seq", "seq", "ch", "seq"]
    counts = {"seq": devices, "ch": groups}
    exchanges = {}
    number = 0
    for n, axis in enumerate(axes):
        send, recv = buffers[2 * n], buffers[2 * n + 1]
        cut = n in (PAIR, RESULT)
        made = []
        for part in range(PARTS if cut else 1):
            ends = (send.at[part], recv.at[part]) if cut else (send, recv)
            made.append(Exchange(number, axis, counts[axis], *ends, send_sem, recv_sem))
            number += 1
        exchanges[n] = made if cut else made[0]
    copies = [
        pltpu.make_async_copy(source, target, input_sem.at[n])
        for n, (source, target) in enumerate(
            zip((*inputs, forward_hbm, inverse_hbm), (*local, forward, inverse))
        )
    ]
    barrier = pltpu.get_barrier_semaphore()
    for exchange in (exchanges[GRAD], exchanges[BACK]):
        for peer in exchange.peers():
            pl.semaphore_signal(
                barrier,
                inc=1,
                device_id={exchange.axis: peer},
                device_id_type=pl.DeviceIdType.MESH,
            )
    for copy in copies:
        copy.start()
    copies[0].wait()
    copies[1].wait()
    pack_part(signal_ref, filter_ref, exchanges[PAIR][0].send, 0)
    pl.semaphore_wait(barrier, devices + groups - 2)
    exchanges[PAIR][0].start()
    for part in range(1, PARTS):
        pack_part(signal_ref, filter_ref, exchanges[PAIR][part].send, part)
        exchanges[PAIR][part].start()
    for copy in copies[2:INPUTS]:
        copy.wait()

    second = second_matrix(w_second_ref, inner)
    back = lax.dot_general(
        d_out_ref[...], second, (((1,), (1,)), ((), ())), preferred_element_type=F32
    ).astype(BF16)
    for c in range(groups):
        exchanges[BACK].send[c] = back[:, c * LANES : (c + 1) * LANES]
    exchanges[BACK].start()
    first[...] = first_matrix(w_first_ref, blocks, inner)
    exchanges[BACK].wait_recv()
    back_ref = exchanges[BACK].recv
    grad_conv_kernel(back_ref, first, gate_ref, exchanges[GRAD].send)
    outer = 2 * (forward.shape[0] - 1)
    exchanges[PAIR][0].wait_recv()
    conv_first(exchanges[PAIR][0].recv, y_ref, 0, outer)
    for part in range(PARTS):
        exchanges[PAIR][part].wait_send()
    exchanges[GRAD].start()
    for part in range(1, PARTS):
        exchanges[PAIR][part].wait_recv()
        conv_first(exchanges[PAIR][part].recv, y_ref, part, outer)
    for copy in copies[INPUTS:]:
        copy.wait()
    conv_kernel(forward, inverse, spec, exchanges[CONV].send, y_ref, z_ref)
    exchanges[CONV].start()
    exchanges[GRAD].wait_recv()
    adjoint_kernel(exchanges[GRAD].recv, spec, forward, inverse, y_ref, z_ref)
    for part in range(PARTS):
        adjoint_last(z_ref, exchanges[RESULT][part].send, part)
        exchanges[RESULT][part].start()
    exchanges[CONV].wait_recv()
    mix_kernel(
        exchanges[CONV].recv,
        back_ref,
        first,
        gate_ref,
        exchanges[MIX].send,
        grad_gate_ref,
        grad_first,
    )
    exchanges[MIX].start()
    exchanges[MIX].wait_recv()
    second_kernel(
        exchanges[MIX].recv, d_out_ref, grad_first, exchanges[SMALL].send, inner, out_block
    )
    exchanges[SMALL].start()
    for part in range(PARTS):
        exchanges[RESULT][part].wait_recv()
        unpack_part(exchanges[RESULT][part].recv, grad_signal_ref, grad_filter_ref, part)
    exchanges[SMALL].wait_recv()
    total = exchanges[SMALL].recv[0]
    for s in range(1, devices):
        total = total + exchanges[SMALL].recv[s]
    small_ref[...] = total
    for n in (BACK, GRAD, CONV, MIX, SMALL):
        exchanges[n].wait_send()
    for exchange in exchanges[RESULT]:
        exchange.wait_send()


def shards_whole(signal, filter_raw, gate, d_out, w_first, w_second):
    rows, width = signal.shape
    devices = lax.axis_size("seq")
    groups = lax.axis_size("ch")
    length = rows * devices
    outer = 2 * length // INNER
    classes = outer // 2 + 1
    forward, inverse = (jnp.asarray(t) for t in dft_tables(outer, float(length) ** (-0.5)))
    blocks, block, _ = w_first.shape
    inner, across, out_block = w_second.shape
    first_rows = blocks * (block // devices) * block // LANES
    second_rows = inner * (across // devices) * out_block // LANES
    small_rows = first_rows + second_rows
    wide = ((PARTS, devices, rows // PARTS, LANES), BF16)
    half = ((devices, rows // 2, LANES), BF16)
    mixed = ((groups, rows, LANES), BF16)
    small = ((devices, small_rows, LANES), F32)
    buffers = [
        pltpu.VMEM(*kind)
        for kind in (wide, mixed, half, half, wide, mixed, small)
        for _ in range(2)
    ]
    vmem = pl.BlockSpec(memory_space=pltpu.VMEM)
    anywhere = pl.BlockSpec(memory_space=pl.ANY)
    field = jax.ShapeDtypeStruct((rows, width), BF16)
    grad_signal, grad_filter, grad_gate, sums = pl.pallas_call(
        functools.partial(whole_kernel, devices, groups, blocks, inner, out_block),
        out_shape=(field, field, field, jax.ShapeDtypeStruct((small_rows, LANES), F32)),
        in_specs=[anywhere] * (INPUTS + 2),
        out_specs=(vmem,) * 4,
        scratch_shapes=buffers
        + [pltpu.VMEM((rows, width), BF16)] * 4
        + [
            pltpu.VMEM((blocks * block, block), BF16),
            pltpu.VMEM((inner * across, out_block), BF16),
            pltpu.VMEM(forward.shape, BF16),
            pltpu.VMEM(inverse.shape, BF16),
            pltpu.VMEM((classes, 2 * INNER, LANES), BF16),
            pltpu.VMEM((classes, 2 * INNER, LANES), BF16),
            pltpu.VMEM((classes, 2 * INNER, LANES), F32),
            pltpu.VMEM((width, width), BF16),
            pltpu.VMEM((devices, first_rows, LANES), F32),
            pltpu.SemaphoreType.DMA((INPUTS + 2,)),
            pltpu.SemaphoreType.DMA((5 + 2 * PARTS, devices)),
            pltpu.SemaphoreType.DMA((5 + 2 * PARTS, devices)),
        ],
        compiler_params=pltpu.CompilerParams(
            collective_id=0, has_side_effects=True, vmem_limit_bytes=60 * 1024 * 1024
        ),
        cost_estimate=pl.CostEstimate(
            flops=20 * 10**9, bytes_accessed=16 * 10**6, transcendentals=0
        ),
    )(
        signal,
        filter_raw,
        gate,
        d_out,
        w_first.reshape(blocks * block, block),
        w_second.reshape(inner * across, out_block),
        forward,
        inverse,
    )
    grad_first = (
        sums[:first_rows]
        .reshape(blocks // 2, block // devices, 2, block)
        .transpose(2, 0, 1, 3)
        .reshape(blocks, block // devices, block)
    )
    grad_second = sums[first_rows:].reshape(inner, across // devices, out_block)
    return (grad_signal, grad_filter, grad_gate, grad_first, grad_second)


def shards(signal, filter_raw, gate, d_out, w_first, w_second):
    rows, width = signal.shape
    devices = lax.axis_size("seq")
    blocks, block, _ = w_first.shape
    inner, across, out_block = w_second.shape
    fits = (
        blocks == devices
        and block == HALF
        and width == devices * HALF
        and width == lax.axis_size("ch") * LANES
        and width == inner * out_block
        and blocks * inner == LANES
        and LANES // out_block == across // devices
        and lax.axis_size("ch") * inner == block
        and devices % lax.axis_size("ch") == 0
        and block // devices == 8
        and rows % (2 * INNER) == 0
        and (rows * devices // INNER) & (rows * devices // INNER - 1) == 0
    )
    body = shards_whole if fits else shards_general
    return body(signal, filter_raw, gate, d_out, w_first, w_second)


def solution(mesh):
    in_specs = (
        P("seq", "ch"),
        P("seq", "ch"),
        P("seq", "ch"),
        P("seq", "ch"),
        P("ch", None, None),
        P("ch", None, None),
    )
    out_specs = (
        P("seq", "ch"),
        P("seq", "ch"),
        P("seq", "ch"),
        P("ch", "seq", None),
        P("ch", "seq", None),
    )
    return jax.shard_map(shards, mesh=mesh, in_specs=in_specs, out_specs=out_specs, check_vma=False)
```

```python
import functools
import math

import jax
import jax.numpy as jnp
import ml_dtypes
import numpy as np
from jax import lax
from jax.experimental import pallas as pl
from jax.experimental.pallas import tpu as pltpu
from jax.sharding import PartitionSpec as P

HIGHEST = lax.Precision.HIGHEST


def counting(count):
    return jnp.arange(count, dtype=jnp.int32)


def phase_table(row_ids, col_ids, length, sign):
    angles = (
        2.0 * math.pi / length * (row_ids[:, None] * col_ids[None, :] % length).astype(jnp.float32)
    )
    return (jnp.cos(angles), sign * jnp.sin(angles))


def contract(form, table, real_part, imag_part):
    cosine, sine = table
    out_real = jnp.einsum(form, cosine, real_part, precision=HIGHEST) - jnp.einsum(
        form, sine, imag_part, precision=HIGHEST
    )
    out_imag = jnp.einsum(form, cosine, imag_part, precision=HIGHEST) + jnp.einsum(
        form, sine, real_part, precision=HIGHEST
    )
    return (out_real, out_imag)


def rotate(cosine, sine, real_part, imag_part):
    return (real_part * cosine - imag_part * sine, real_part * sine + imag_part * cosine)


def factors(length):
    return (length // 128, 128)


def local_forward(real_part, imag_part):
    fields, group, rows, width = real_part.shape
    outer, inner = factors(rows)
    real_part = real_part.reshape(fields, group, outer, inner, width)
    imag_part = imag_part.reshape(fields, group, outer, inner, width)
    real_part, imag_part = contract(
        "qa,fkabc->fkqbc",
        phase_table(counting(outer), counting(outer), outer, -1.0),
        real_part,
        imag_part,
    )
    cosine, sine = phase_table(counting(outer), counting(inner), rows, -1.0)
    real_part, imag_part = rotate(cosine[:, :, None], sine[:, :, None], real_part, imag_part)
    return contract(
        "rb,fkqbc->fkqrc",
        phase_table(counting(inner), counting(inner), inner, -1.0),
        real_part,
        imag_part,
    )


def local_inverse(real_part, imag_part):
    fields, group, outer, inner, width = real_part.shape
    rows = outer * inner
    real_part, imag_part = contract(
        "br,fkqrc->fkqbc",
        phase_table(counting(inner), counting(inner), inner, 1.0),
        real_part,
        imag_part,
    )
    cosine, sine = phase_table(counting(outer), counting(inner), rows, 1.0)
    real_part, imag_part = rotate(cosine[:, :, None], sine[:, :, None], real_part, imag_part)
    real_part, imag_part = contract(
        "aq,fkqbc->fkabc",
        phase_table(counting(outer), counting(outer), outer, 1.0),
        real_part,
        imag_part,
    )
    return (
        real_part.reshape(fields, group, rows, width),
        imag_part.reshape(fields, group, rows, width),
    )


def forward_transform(fields):
    devices = lax.axis_size("seq")
    count, rows, width = fields.shape
    piece = rows // devices
    span = 2 * devices
    whole = span * rows
    parts = lax.all_to_all(fields[:, None], "seq", split_axis=2, concat_axis=1, tiled=True)
    cosine, sine = phase_table(counting(span), counting(devices), span, -1.0)
    real_part = jnp.einsum("ka,fabc->fkbc", cosine, parts, precision=HIGHEST)
    imag_part = jnp.einsum("ka,fabc->fkbc", sine, parts, precision=HIGHEST)
    positions = lax.axis_index("seq") * piece + counting(piece)
    cosine, sine = phase_table(counting(span), positions, whole, -1.0)
    real_part, imag_part = rotate(cosine[:, :, None], sine[:, :, None], real_part, imag_part)
    spectrum = lax.all_to_all(
        jnp.stack([real_part, imag_part], axis=1), "seq", split_axis=2, concat_axis=3, tiled=True
    )
    return local_forward(spectrum[:, 0], spectrum[:, 1])


def inverse_transform(real_part, imag_part):
    devices = lax.axis_size("seq")
    real_part, imag_part = local_inverse(real_part, imag_part)
    group = real_part.shape[1]
    rows = real_part.shape[2]
    span = 2 * devices
    whole = span * rows
    classes = lax.axis_index("seq") * group + counting(group)
    cosine, sine = phase_table(classes, counting(rows), whole, 1.0)
    real_part, imag_part = rotate(cosine[:, :, None], sine[:, :, None], real_part, imag_part)
    gathered = lax.all_to_all(
        jnp.stack([real_part, imag_part], axis=1), "seq", split_axis=3, concat_axis=2, tiled=True
    )
    cosine, sine = phase_table(counting(devices), counting(span), span, 1.0)
    inverse_scale = 1.0 / whole
    out_real = (
        jnp.einsum("ak,fkbc->fabc", cosine, gathered[:, 0], precision=HIGHEST)
        - jnp.einsum("ak,fkbc->fabc", sine, gathered[:, 1], precision=HIGHEST)
    ) * inverse_scale
    slab = lax.all_to_all(out_real, "seq", split_axis=1, concat_axis=2, tiled=True)
    return slab[:, 0]


def adjoint_spectra(spectra_real, spectra_imag, incoming_real, incoming_imag):
    toward_signal_real = spectra_real[1] * incoming_real + spectra_imag[1] * incoming_imag
    toward_signal_imag = spectra_real[1] * incoming_imag - spectra_imag[1] * incoming_real
    toward_filter_real = spectra_real[0] * incoming_real + spectra_imag[0] * incoming_imag
    toward_filter_imag = spectra_real[0] * incoming_imag - spectra_imag[0] * incoming_real
    return (toward_signal_real, toward_signal_imag, toward_filter_real, toward_filter_imag)


def shards_general(signal, filter_raw, gate, d_out, w_first, w_second):
    rows, width = signal.shape
    scale = float(rows * lax.axis_size("seq")) ** (-0.5)
    signal_wide = signal.astype(jnp.float32)
    kernel = filter_raw.astype(jnp.float32) * scale
    spectra_real, spectra_imag = forward_transform(jnp.stack([signal_wide, kernel]))
    mixed_real = spectra_real[0] * spectra_real[1] - spectra_imag[0] * spectra_imag[1]
    mixed_imag = spectra_real[0] * spectra_imag[1] + spectra_imag[0] * spectra_real[1]
    conv = inverse_transform(mixed_real[None], mixed_imag[None])[0].astype(jnp.bfloat16)
    gate_wide = gate.astype(jnp.float32)
    product = (conv.astype(jnp.float32) * gate_wide).astype(jnp.bfloat16)
    blocks = w_first.shape[0]
    block = w_first.shape[1]
    product_blocks = product.reshape(rows, blocks, block)
    first_mix = jnp.einsum(
        "tij,ijk->tik", product_blocks, w_first, preferred_element_type=jnp.float32
    ).astype(jnp.bfloat16)
    received = lax.all_to_all(first_mix, "ch", split_axis=2, concat_axis=1, tiled=True)
    incoming = d_out.reshape(rows, w_second.shape[0], w_second.shape[1])
    second_back = jnp.einsum(
        "tko,kio->tki", incoming, w_second, preferred_element_type=jnp.float32
    ).astype(jnp.bfloat16)
    grad_second = jnp.einsum("tik,tko->kio", received, incoming, preferred_element_type=jnp.float32)
    returned = lax.all_to_all(second_back, "ch", split_axis=2, concat_axis=1, tiled=True)
    grad_product = jnp.einsum(
        "tki,ijk->tij", returned, w_first, preferred_element_type=jnp.float32
    ).reshape(rows, width)
    grad_first = jnp.einsum(
        "tij,tki->ijk", product_blocks, returned, preferred_element_type=jnp.float32
    )
    grad_gate = (grad_product * conv.astype(jnp.float32)).astype(jnp.bfloat16)
    grad_conv = grad_product * gate_wide
    incoming_real, incoming_imag = forward_transform(grad_conv[None])
    sig_real, sig_imag, fil_real, fil_imag = adjoint_spectra(
        spectra_real, spectra_imag, incoming_real[0], incoming_imag[0]
    )
    results = inverse_transform(jnp.stack([sig_real, fil_real]), jnp.stack([sig_imag, fil_imag]))
    grad_signal = results[0].astype(jnp.bfloat16)
    grad_filter = (results[1] * scale).astype(jnp.bfloat16)
    grad_first = lax.psum_scatter(
        grad_first.astype(jnp.bfloat16), "seq", scatter_dimension=1, tiled=True
    ).astype(jnp.float32)
    grad_second = lax.psum_scatter(grad_second, "seq", scatter_dimension=1, tiled=True)
    return (grad_signal, grad_filter, grad_gate, grad_first, grad_second)


F32 = jnp.float32
BF16 = jnp.bfloat16
LANES = 128
HALF = 64
INNER = 128
CHUNK = 16
PARTS = 2


def dft_tables(outer, scale):
    length = outer * INNER
    q = np.arange(outer // 2 + 1)[:, None, None]
    r = np.arange(INNER)[None, :, None]
    b = np.arange(INNER)[None, None, :]
    angle = 2.0 * np.pi / length * ((b * (q + outer * r)) % length)
    c, s = np.cos(angle), np.sin(angle)
    forward = np.concatenate(
        [np.concatenate([c, s], axis=2), np.concatenate([-s, c], axis=2)], axis=1
    )
    inverse = forward.transpose(0, 2, 1) * (scale / length)
    return forward.astype(ml_dtypes.bfloat16), inverse.astype(ml_dtypes.bfloat16)


def times(value, cosine, sine):
    real, imag = value
    if imag is None:
        return (real * cosine, real * sine)
    return (real * cosine - imag * sine, real * sine + imag * cosine)


def real_dft(values, length):
    if length == 2:
        return [(values[0], None), (values[0], None)]
    even = real_dft(values[0::2], length // 2)
    odd = real_dft(values[1::2], length // 2)
    half, quarter = length // 2, length // 4
    out = [None] * (half + 1)
    for q in range(quarter + 1):
        er, ei = even[q]
        if q == 0:
            out[0] = (er + odd[0][0], None)
            out[half] = (er - odd[0][0], None)
        elif q == quarter:
            out[q] = (er, -odd[q][0])
        else:
            angle = 2.0 * math.pi * q / length
            tr, ti = times(odd[q], math.cos(angle), -math.sin(angle))
            out[q] = (er + tr, ei + ti)
            out[half - q] = (er - tr, ti - ei)
    return out


def real_inverse(values, length):
    if length == 2:
        return [values[0][0] + values[1][0]]
    half, quarter = length // 2, length // 4
    even, odd = [], []
    for q in range(quarter + 1):
        zr, zi = values[q]
        if q == 0:
            wr = values[half][0]
            even.append((zr + wr, None))
            odd.append((zr - wr, None))
        elif q == quarter:
            even.append((zr + zr, None))
            odd.append((-(zi + zi), None))
        else:
            wr, wi = values[half - q]
            even.append((zr + wr, zi - wi))
            angle = 2.0 * math.pi * q / length
            odd.append(times((zr - wr, zi + wi), math.cos(angle), math.sin(angle)))
    out = [None] * half
    out[0::2] = real_inverse(even, half)
    out[1::2] = real_inverse(odd, half)
    return out


def low_lanes(rows):
    return lax.broadcasted_iota(jnp.int32, (rows, LANES), 1) < HALF


def swap(value):
    return pltpu.roll(value, HALF, 1)


def store_classes(y_ref, rows, spectrum):
    for q, (real, imag) in enumerate(spectrum):
        y_ref[q, pl.ds(rows, CHUNK), :] = real.astype(BF16)
        imag = jnp.zeros_like(real) if imag is None else imag
        y_ref[q, pl.ds(INNER + rows, CHUNK), :] = imag.astype(BF16)


def load_classes(z_ref, rows, classes):
    out = []
    for q in range(classes):
        real = z_ref[q, pl.ds(rows, CHUNK), :]
        edge = q == 0 or q == classes - 1
        out.append((real, None if edge else z_ref[q, pl.ds(INNER + rows, CHUNK), :]))
    return out


def pack_part(signal_ref, filter_ref, out_ref, part):
    size = INNER // PARTS
    low = low_lanes(size)
    for p in range(out_ref.shape[0] // 2):
        cols = slice(p * LANES, (p + 1) * LANES)
        for m in range(signal_ref.shape[0] // INNER):
            source = slice(m * INNER + part * size, m * INNER + (part + 1) * size)
            rows = slice(m * size, (m + 1) * size)
            a = signal_ref[source, cols].astype(F32)
            b = filter_ref[source, cols].astype(F32)
            out_ref[2 * p, rows, :] = jnp.where(low, a, swap(b)).astype(BF16)
            out_ref[2 * p + 1, rows, :] = jnp.where(low, swap(a), b).astype(BF16)


def unpack_part(in_ref, signal_ref, filter_ref, part):
    size = INNER // PARTS
    low = low_lanes(size)
    for p in range(in_ref.shape[0] // 2):
        cols = slice(p * LANES, (p + 1) * LANES)
        for m in range(signal_ref.shape[0] // INNER):
            target = slice(m * INNER + part * size, m * INNER + (part + 1) * size)
            rows = slice(m * size, (m + 1) * size)
            a = in_ref[2 * p, rows, :].astype(F32)
            b = in_ref[2 * p + 1, rows, :].astype(F32)
            filter_ref[target, cols] = jnp.where(low, a, swap(b)).astype(BF16)
            signal_ref[target, cols] = jnp.where(low, swap(a), b).astype(BF16)


def conv_first(pair_ref, y_ref, part, outer):
    size = INNER // PARTS
    tiles = outer // 2 // pair_ref.shape[0]

    def first(j, carry):
        at = pl.multiple_of(j * CHUNK, CHUNK)
        points = [
            pair_ref[a // tiles, pl.ds((a % tiles) * size + at, CHUNK), :].astype(F32)
            for a in range(outer // 2)
        ]
        store_classes(y_ref, part * size + at, real_dft(points, outer))
        return carry

    lax.fori_loop(0, size // CHUNK, first, 0)


def conv_kernel(forward_ref, inverse_ref, spec_ref, conv_ref, y_ref, z_ref):
    devices, packed, _ = conv_ref.shape
    classes = forward_ref.shape[0]
    outer = 2 * (classes - 1)
    tiles = 2 * packed // INNER

    def middle(q, carry):
        x = jnp.dot(forward_ref[q], y_ref[q], preferred_element_type=F32)
        spec_ref[q] = x.astype(BF16)
        o = swap(x)
        xr, xi, orr, oi = x[:INNER], x[INNER:], o[:INNER], o[INNER:]
        mixed = jnp.concatenate([xr * orr - xi * oi, xr * oi + xi * orr], axis=0)
        z_ref[q] = jnp.dot(inverse_ref[q], mixed.astype(BF16), preferred_element_type=F32)
        return carry

    lax.fori_loop(0, classes, middle, 0, unroll=11)
    low = low_lanes(CHUNK)
    halves = tiles // 2

    def last(j, carry):
        at = pl.multiple_of(j * CHUNK, CHUNK)
        points = real_inverse(load_classes(z_ref, at, classes), outer)
        for s in range(devices):
            for m in range(halves):
                a = s * tiles + m
                value = jnp.where(low, points[a], points[a + halves])
                conv_ref[s, pl.ds(m * INNER + at, CHUNK), :] = value.astype(BF16)
        return carry

    lax.fori_loop(0, INNER // CHUNK, last, 0)


def adjoint_kernel(grad_ref, spec_ref, forward_ref, inverse_ref, y_ref, z_ref):
    devices, packed, _ = grad_ref.shape
    classes = forward_ref.shape[0]
    outer = 2 * (classes - 1)
    halves = packed // INNER
    tiles = 2 * halves
    low = low_lanes(CHUNK)

    def first(j, carry):
        at = pl.multiple_of(j * CHUNK, CHUNK)
        points = [None] * (outer // 2)
        for s in range(devices):
            for m in range(halves):
                value = grad_ref[s, pl.ds(m * INNER + at, CHUNK), :].astype(F32)
                other = swap(value)
                points[s * tiles + m] = jnp.where(low, value, other)
                points[s * tiles + halves + m] = jnp.where(low, other, value)
        store_classes(y_ref, at, real_dft(points, outer))
        return carry

    lax.fori_loop(0, INNER // CHUNK, first, 0)

    def middle(q, carry):
        g = jnp.dot(forward_ref[q], y_ref[q], preferred_element_type=F32)
        x = spec_ref[q].astype(F32)
        gr, gi, xr, xi = g[:INNER], g[INNER:], x[:INNER], x[INNER:]
        mixed = jnp.concatenate([xr * gr + xi * gi, xr * gi - xi * gr], axis=0)
        z_ref[q] = jnp.dot(inverse_ref[q], mixed.astype(BF16), preferred_element_type=F32)
        return carry

    lax.fori_loop(0, classes, middle, 0, unroll=11)


def adjoint_last(z_ref, out_ref, part):
    size = INNER // PARTS
    classes = z_ref.shape[0]
    outer = 2 * (classes - 1)
    tiles = outer // 2 // out_ref.shape[0]

    def last(j, carry):
        at = pl.multiple_of(j * CHUNK, CHUNK)
        points = real_inverse(load_classes(z_ref, part * size + at, classes), outer)
        for a in range(outer // 2):
            rows = pl.ds((a % tiles) * size + at, CHUNK)
            out_ref[a // tiles, rows, :] = points[a].astype(BF16)
        return carry

    lax.fori_loop(0, size // CHUNK, last, 0)


def joined(ref):
    return jnp.concatenate([ref[c] for c in range(ref.shape[0])], axis=1)


def grad_product_of(back, first):
    return lax.dot_general(back, first, (((1,), (1,)), ((), ())), preferred_element_type=F32)


def grad_conv_kernel(back_ref, first_ref, gate_ref, out_ref):
    value = grad_product_of(joined(back_ref), first_ref[...]) * gate_ref[...].astype(F32)
    half = value.shape[0] // 2
    low = low_lanes(half)
    for p in range(out_ref.shape[0] // 2):
        top = value[:half, p * LANES : (p + 1) * LANES]
        bottom = value[half:, p * LANES : (p + 1) * LANES]
        out_ref[2 * p] = jnp.where(low, top, swap(bottom)).astype(BF16)
        out_ref[2 * p + 1] = jnp.where(low, swap(top), bottom).astype(BF16)


def mix_kernel(conv_ref, back_ref, first_ref, gate_ref, mix_ref, grad_gate_ref, grad_first_ref):
    devices, half, _ = conv_ref.shape
    low = low_lanes(half)
    parts = []
    for p in range(devices // 2):
        a = conv_ref[2 * p].astype(F32)
        b = conv_ref[2 * p + 1].astype(F32)
        parts.append(
            jnp.concatenate([jnp.where(low, a, swap(b)), jnp.where(low, swap(a), b)], axis=0)
        )
    conv = jnp.concatenate(parts, axis=1)
    product = (conv * gate_ref[...].astype(F32)).astype(BF16)
    first = first_ref[...]
    mix = jnp.dot(product, first, preferred_element_type=F32).astype(BF16)
    groups = mix_ref.shape[0]
    for c in range(groups):
        mix_ref[c] = mix[:, c * LANES : (c + 1) * LANES]
    back = joined(back_ref)
    grad_gate_ref[...] = (grad_product_of(back, first) * conv).astype(BF16)
    whole = lax.dot_general(product, back, (((0,), (0,)), ((), ())), preferred_element_type=F32)
    count = whole.shape[0]
    lane = lax.broadcasted_iota(jnp.int32, (count, LANES), 1)
    row = lax.broadcasted_iota(jnp.int32, (count, LANES), 0)
    inner = LANES // devices
    keep = lane // inner == row // (count // devices)
    grads = jnp.zeros((count, LANES), F32)
    for c in range(groups):
        value = jnp.where(keep, whole[:, c * LANES : (c + 1) * LANES], 0.0)
        shift = inner
        while shift < LANES:
            value = value + pltpu.roll(value, shift, 1)
            shift *= 2
        grads = jnp.where((lane // inner) % groups == c, value, grads)
    block = count // devices
    piece = block // devices
    pairs = devices // 2
    small = low_lanes(piece)
    for i in range(pairs):
        for s in range(devices):
            a = grads[i * block + s * piece : i * block + (s + 1) * piece]
            k = i + pairs
            b = grads[k * block + s * piece : k * block + (s + 1) * piece]
            grad_first_ref[s, i * piece : (i + 1) * piece, :] = jnp.where(small, a, b)


def second_kernel(mix_ref, d_out_ref, grad_first_ref, out_ref, inner, width):
    groups = mix_ref.shape[0]
    devices, first_rows, _ = grad_first_ref.shape
    out_ref[:, :first_rows, :] = grad_first_ref[...]
    d_out = d_out_ref[...]
    lane = lax.broadcasted_iota(jnp.int32, (LANES, LANES), 1)
    row = lax.broadcasted_iota(jnp.int32, (LANES, LANES), 0)
    folds = LANES // width
    per = devices // groups
    slot = lax.broadcasted_iota(jnp.int32, (inner, LANES), 1) // width
    for c in range(groups):
        whole = lax.dot_general(
            mix_ref[c], d_out, (((0,), (0,)), ((), ())), preferred_element_type=F32
        )
        total = jnp.zeros((LANES, LANES), F32)
        for g in range(whole.shape[1] // LANES):
            keep = lane // width + g * folds == row % inner
            total = total + jnp.where(keep, whole[:, g * LANES : (g + 1) * LANES], 0.0)
        shift = width
        while shift < LANES:
            total = total + pltpu.roll(total, shift, 1)
            shift *= 2
        for d in range(per):
            base = d * folds * inner
            piece = jnp.zeros((inner, LANES), F32)
            for i in range(folds):
                piece = jnp.where(slot == i, total[base + i * inner : base + (i + 1) * inner], piece)
            out_ref[c * per + d, first_rows:, :] = piece


PAIR, BACK, GRAD, CONV, RESULT, MIX, SMALL = range(7)
INPUTS = 6


class Exchange:
    def __init__(self, number, axis, count, send, recv, send_sem, recv_sem):
        self.axis, self.count, self.send, self.recv = axis, count, send, recv
        self.number, self.send_sem, self.recv_sem = number, send_sem, recv_sem
        self.me = lax.axis_index(axis)

    def copy(self, peer, slot):
        return pltpu.make_async_remote_copy(
            src_ref=self.send.at[peer],
            dst_ref=self.recv.at[slot],
            send_sem=self.send_sem.at[self.number, peer],
            recv_sem=self.recv_sem.at[self.number, slot],
            device_id={self.axis: peer},
            device_id_type=pl.DeviceIdType.MESH,
        )

    def peers(self):
        half = self.count // 2
        own = half * (self.me // half)
        far = [half - own + lax.rem(self.me + d, half) for d in range(half)]
        return far + [own + lax.rem(self.me + d, half) for d in range(1, half)]

    def start(self):
        for peer in self.peers():
            self.copy(peer, self.me).start()
        self.recv[self.me] = self.send[self.me]

    def wait_recv(self):
        for peer in self.peers():
            self.copy(peer, peer).wait_recv()

    def wait_send(self):
        for peer in self.peers():
            self.copy(peer, self.me).wait_send()


def spread(values, pick):
    return jnp.dot(values, pick.astype(F32).astype(BF16), preferred_element_type=F32)


def first_matrix(w_ref, blocks, inner):
    rows, block = w_ref.shape
    shape = (block, rows)
    k = lax.broadcasted_iota(jnp.int32, shape, 0)
    col = lax.broadcasted_iota(jnp.int32, shape, 1)
    wide = spread(w_ref[...], k == (col // LANES) * inner + col % inner)
    row = lax.broadcasted_iota(jnp.int32, wide.shape, 0)
    col = lax.broadcasted_iota(jnp.int32, wide.shape, 1)
    return jnp.where(row // block == (col % LANES) // inner, wide, 0.0).astype(BF16)


def second_matrix(w_ref, inner):
    rows, width = w_ref.shape
    across = rows // inner
    r = lax.broadcasted_iota(jnp.int32, (rows, rows), 0)
    c = lax.broadcasted_iota(jnp.int32, (rows, rows), 1)
    order = (c == (r % inner) * across + r // inner).astype(F32).astype(BF16)
    turned = jnp.dot(order, w_ref[...], preferred_element_type=F32).astype(BF16)
    o = lax.broadcasted_iota(jnp.int32, (width, inner * width), 0)
    c = lax.broadcasted_iota(jnp.int32, (width, inner * width), 1)
    wide = spread(turned, o == c % width)
    row = lax.broadcasted_iota(jnp.int32, wide.shape, 0)
    col = lax.broadcasted_iota(jnp.int32, wide.shape, 1)
    return jnp.where(row % inner == col // width, wide, 0.0).astype(BF16)


def whole_kernel(
    devices,
    groups,
    blocks,
    inner,
    out_block,
    *refs,
):
    inputs, (forward_hbm, inverse_hbm) = refs[:INPUTS], refs[INPUTS : INPUTS + 2]
    refs = refs[INPUTS + 2 :]
    grad_signal_ref, grad_filter_ref, grad_gate_ref, small_ref = refs[:4]
    buffers, local, rest = refs[4:18], refs[18 : 18 + INPUTS], refs[18 + INPUTS :]
    (forward, inverse, spec, y_ref, z_ref, first, grad_first) = rest[:7]
    input_sem, send_sem, recv_sem = rest[7:]
    signal_ref, filter_ref, gate_ref, d_out_ref, w_first_ref, w_second_ref = local
    axes = ["seq", "ch", "seq", "seq", "seq", "ch", "seq"]
    counts = {"seq": devices, "ch": groups}
    exchanges = {}
    number = 0
    for n, axis in enumerate(axes):
        send, recv = buffers[2 * n], buffers[2 * n + 1]
        cut = n in (PAIR, RESULT)
        made = []
        for part in range(PARTS if cut else 1):
            ends = (send.at[part], recv.at[part]) if cut else (send, recv)
            made.append(Exchange(number, axis, counts[axis], *ends, send_sem, recv_sem))
            number += 1
        exchanges[n] = made if cut else made[0]
    copies = [
        pltpu.make_async_copy(source, target, input_sem.at[n])
        for n, (source, target) in enumerate(
            zip((*inputs, forward_hbm, inverse_hbm), (*local, forward, inverse))
        )
    ]
    barrier = pltpu.get_barrier_semaphore()
    for exchange in (exchanges[GRAD], exchanges[BACK]):
        for peer in exchange.peers():
            pl.semaphore_signal(
                barrier,
                inc=1,
                device_id={exchange.axis: peer},
                device_id_type=pl.DeviceIdType.MESH,
            )
    for copy in copies:
        copy.start()
    copies[0].wait()
    copies[1].wait()
    pack_part(signal_ref, filter_ref, exchanges[PAIR][0].send, 0)
    pl.semaphore_wait(barrier, devices + groups - 2)
    exchanges[PAIR][0].start()
    for part in range(1, PARTS):
        pack_part(signal_ref, filter_ref, exchanges[PAIR][part].send, part)
        exchanges[PAIR][part].start()
    for copy in copies[2:INPUTS]:
        copy.wait()

    second = second_matrix(w_second_ref, inner)
    back = lax.dot_general(
        d_out_ref[...], second, (((1,), (1,)), ((), ())), preferred_element_type=F32
    ).astype(BF16)
    for c in range(groups):
        exchanges[BACK].send[c] = back[:, c * LANES : (c + 1) * LANES]
    exchanges[BACK].start()
    first[...] = first_matrix(w_first_ref, blocks, inner)
    exchanges[BACK].wait_recv()
    back_ref = exchanges[BACK].recv
    grad_conv_kernel(back_ref, first, gate_ref, exchanges[GRAD].send)
    outer = 2 * (forward.shape[0] - 1)
    exchanges[PAIR][0].wait_recv()
    conv_first(exchanges[PAIR][0].recv, y_ref, 0, outer)
    for part in range(PARTS):
        exchanges[PAIR][part].wait_send()
    exchanges[GRAD].start()
    for part in range(1, PARTS):
        exchanges[PAIR][part].wait_recv()
        conv_first(exchanges[PAIR][part].recv, y_ref, part, outer)
    for copy in copies[INPUTS:]:
        copy.wait()
    conv_kernel(forward, inverse, spec, exchanges[CONV].send, y_ref, z_ref)
    exchanges[CONV].start()
    exchanges[GRAD].wait_recv()
    adjoint_kernel(exchanges[GRAD].recv, spec, forward, inverse, y_ref, z_ref)
    for part in range(PARTS):
        adjoint_last(z_ref, exchanges[RESULT][part].send, part)
        exchanges[RESULT][part].start()
    exchanges[CONV].wait_recv()
    mix_kernel(
        exchanges[CONV].recv,
        back_ref,
        first,
        gate_ref,
        exchanges[MIX].send,
        grad_gate_ref,
        grad_first,
    )
    exchanges[MIX].start()
    exchanges[MIX].wait_recv()
    second_kernel(
        exchanges[MIX].recv, d_out_ref, grad_first, exchanges[SMALL].send, inner, out_block
    )
    exchanges[SMALL].start()
    for part in range(PARTS):
        exchanges[RESULT][part].wait_recv()
        unpack_part(exchanges[RESULT][part].recv, grad_signal_ref, grad_filter_ref, part)
    exchanges[SMALL].wait_recv()
    total = exchanges[SMALL].recv[0]
    for s in range(1, devices):
        total = total + exchanges[SMALL].recv[s]
    small_ref[...] = total
    for n in (BACK, GRAD, CONV, MIX, SMALL):
        exchanges[n].wait_send()
    for exchange in exchanges[RESULT]:
        exchange.wait_send()


def finish_kernel(
    signal_ref, filter_ref, gate_ref, small_ref, signal_out, filter_out, gate_out, first_out, second_out
):
    signal_out[...] = signal_ref[...]
    filter_out[...] = filter_ref[...]
    gate_out[...] = gate_ref[...]
    blocks, piece, block = first_out.shape
    pairs = blocks // 2
    for i in range(pairs):
        value = small_ref[i * piece : (i + 1) * piece, :]
        first_out[i] = value[:, :block]
        first_out[i + pairs] = swap(value)[:, :block]
    inner, across, width = second_out.shape
    value = small_ref[pairs * piece :, :]
    for i in range(across):
        part = value if i == 0 else pltpu.roll(value, LANES - i * width, 1)
        for k in range(inner):
            second_out[k, i : i + 1, :] = part[k : k + 1, :width]


def shards_whole(signal, filter_raw, gate, d_out, w_first, w_second):
    rows, width = signal.shape
    devices = lax.axis_size("seq")
    groups = lax.axis_size("ch")
    length = rows * devices
    outer = 2 * length // INNER
    classes = outer // 2 + 1
    forward, inverse = (jnp.asarray(t) for t in dft_tables(outer, float(length) ** (-0.5)))
    blocks, block, _ = w_first.shape
    inner, across, out_block = w_second.shape
    first_rows = blocks * (block // devices) * block // LANES
    second_rows = inner * (across // devices) * out_block // LANES
    small_rows = first_rows + second_rows
    wide = ((PARTS, devices, rows // PARTS, LANES), BF16)
    half = ((devices, rows // 2, LANES), BF16)
    mixed = ((groups, rows, LANES), BF16)
    small = ((devices, small_rows, LANES), F32)
    buffers = [
        pltpu.VMEM(*kind)
        for kind in (wide, mixed, half, half, wide, mixed, small)
        for _ in range(2)
    ]
    vmem = pl.BlockSpec(memory_space=pltpu.VMEM)
    anywhere = pl.BlockSpec(memory_space=pl.ANY)
    field = jax.ShapeDtypeStruct((rows, width), BF16)
    grad_signal, grad_filter, grad_gate, sums = pl.pallas_call(
        functools.partial(whole_kernel, devices, groups, blocks, inner, out_block),
        out_shape=(field, field, field, jax.ShapeDtypeStruct((small_rows, LANES), F32)),
        in_specs=[anywhere] * (INPUTS + 2),
        out_specs=(vmem,) * 4,
        scratch_shapes=buffers
        + [pltpu.VMEM((rows, width), BF16)] * 4
        + [
            pltpu.VMEM((blocks * block, block), BF16),
            pltpu.VMEM((inner * across, out_block), BF16),
            pltpu.VMEM(forward.shape, BF16),
            pltpu.VMEM(inverse.shape, BF16),
            pltpu.VMEM((classes, 2 * INNER, LANES), BF16),
            pltpu.VMEM((classes, 2 * INNER, LANES), BF16),
            pltpu.VMEM((classes, 2 * INNER, LANES), F32),
            pltpu.VMEM((width, width), BF16),
            pltpu.VMEM((devices, first_rows, LANES), F32),
            pltpu.SemaphoreType.DMA((INPUTS + 2,)),
            pltpu.SemaphoreType.DMA((5 + 2 * PARTS, devices)),
            pltpu.SemaphoreType.DMA((5 + 2 * PARTS, devices)),
        ],
        compiler_params=pltpu.CompilerParams(
            collective_id=0, has_side_effects=True, vmem_limit_bytes=60 * 1024 * 1024
        ),
        cost_estimate=pl.CostEstimate(
            flops=20 * 10**9, bytes_accessed=16 * 10**6, transcendentals=0
        ),
    )(
        signal,
        filter_raw,
        gate,
        d_out,
        w_first.reshape(blocks * block, block),
        w_second.reshape(inner * across, out_block),
        forward,
        inverse,
    )
    shape = jax.ShapeDtypeStruct
    return pl.pallas_call(
        finish_kernel,
        out_shape=(
            field,
            field,
            field,
            shape((blocks, block // devices, block), F32),
            shape((inner, across // devices, out_block), F32),
        ),
        compiler_params=pltpu.CompilerParams(vmem_limit_bytes=60 * 1024 * 1024),
    )(grad_signal, grad_filter, grad_gate, sums)


def shards(signal, filter_raw, gate, d_out, w_first, w_second):
    rows, width = signal.shape
    devices = lax.axis_size("seq")
    blocks, block, _ = w_first.shape
    inner, across, out_block = w_second.shape
    fits = (
        blocks == devices
        and block == HALF
        and width == devices * HALF
        and width == lax.axis_size("ch") * LANES
        and width == inner * out_block
        and blocks * inner == LANES
        and LANES // out_block == across // devices
        and lax.axis_size("ch") * inner == block
        and devices % lax.axis_size("ch") == 0
        and block // devices == 8
        and rows % (2 * INNER) == 0
        and (rows * devices // INNER) & (rows * devices // INNER - 1) == 0
    )
    body = shards_whole if fits else shards_general
    return body(signal, filter_raw, gate, d_out, w_first, w_second)


def solution(mesh):
    in_specs = (
        P("seq", "ch"),
        P("seq", "ch"),
        P("seq", "ch"),
        P("seq", "ch"),
        P("ch", None, None),
        P("ch", None, None),
    )
    out_specs = (
        P("seq", "ch"),
        P("seq", "ch"),
        P("seq", "ch"),
        P("ch", "seq", None),
        P("ch", "seq", None),
    )
    return jax.shard_map(shards, mesh=mesh, in_specs=in_specs, out_specs=out_specs, check_vma=False)
```

```python
import functools
import math

import jax
import jax.numpy as jnp
import ml_dtypes
import numpy as np
from jax import lax
from jax.experimental import pallas as pl
from jax.experimental.pallas import tpu as pltpu
from jax.sharding import PartitionSpec as P

HIGHEST = lax.Precision.HIGHEST


def counting(count):
    return jnp.arange(count, dtype=jnp.int32)


def phase_table(row_ids, col_ids, length, sign):
    angles = (
        2.0 * math.pi / length * (row_ids[:, None] * col_ids[None, :] % length).astype(jnp.float32)
    )
    return (jnp.cos(angles), sign * jnp.sin(angles))


def contract(form, table, real_part, imag_part):
    cosine, sine = table
    out_real = jnp.einsum(form, cosine, real_part, precision=HIGHEST) - jnp.einsum(
        form, sine, imag_part, precision=HIGHEST
    )
    out_imag = jnp.einsum(form, cosine, imag_part, precision=HIGHEST) + jnp.einsum(
        form, sine, real_part, precision=HIGHEST
    )
    return (out_real, out_imag)


def rotate(cosine, sine, real_part, imag_part):
    return (real_part * cosine - imag_part * sine, real_part * sine + imag_part * cosine)


def factors(length):
    return (length // 128, 128)


def local_forward(real_part, imag_part):
    fields, group, rows, width = real_part.shape
    outer, inner = factors(rows)
    real_part = real_part.reshape(fields, group, outer, inner, width)
    imag_part = imag_part.reshape(fields, group, outer, inner, width)
    real_part, imag_part = contract(
        "qa,fkabc->fkqbc",
        phase_table(counting(outer), counting(outer), outer, -1.0),
        real_part,
        imag_part,
    )
    cosine, sine = phase_table(counting(outer), counting(inner), rows, -1.0)
    real_part, imag_part = rotate(cosine[:, :, None], sine[:, :, None], real_part, imag_part)
    return contract(
        "rb,fkqbc->fkqrc",
        phase_table(counting(inner), counting(inner), inner, -1.0),
        real_part,
        imag_part,
    )


def local_inverse(real_part, imag_part):
    fields, group, outer, inner, width = real_part.shape
    rows = outer * inner
    real_part, imag_part = contract(
        "br,fkqrc->fkqbc",
        phase_table(counting(inner), counting(inner), inner, 1.0),
        real_part,
        imag_part,
    )
    cosine, sine = phase_table(counting(outer), counting(inner), rows, 1.0)
    real_part, imag_part = rotate(cosine[:, :, None], sine[:, :, None], real_part, imag_part)
    real_part, imag_part = contract(
        "aq,fkqbc->fkabc",
        phase_table(counting(outer), counting(outer), outer, 1.0),
        real_part,
        imag_part,
    )
    return (
        real_part.reshape(fields, group, rows, width),
        imag_part.reshape(fields, group, rows, width),
    )


def forward_transform(fields):
    devices = lax.axis_size("seq")
    count, rows, width = fields.shape
    piece = rows // devices
    span = 2 * devices
    whole = span * rows
    parts = lax.all_to_all(fields[:, None], "seq", split_axis=2, concat_axis=1, tiled=True)
    cosine, sine = phase_table(counting(span), counting(devices), span, -1.0)
    real_part = jnp.einsum("ka,fabc->fkbc", cosine, parts, precision=HIGHEST)
    imag_part = jnp.einsum("ka,fabc->fkbc", sine, parts, precision=HIGHEST)
    positions = lax.axis_index("seq") * piece + counting(piece)
    cosine, sine = phase_table(counting(span), positions, whole, -1.0)
    real_part, imag_part = rotate(cosine[:, :, None], sine[:, :, None], real_part, imag_part)
    spectrum = lax.all_to_all(
        jnp.stack([real_part, imag_part], axis=1), "seq", split_axis=2, concat_axis=3, tiled=True
    )
    return local_forward(spectrum[:, 0], spectrum[:, 1])


def inverse_transform(real_part, imag_part):
    devices = lax.axis_size("seq")
    real_part, imag_part = local_inverse(real_part, imag_part)
    group = real_part.shape[1]
    rows = real_part.shape[2]
    span = 2 * devices
    whole = span * rows
    classes = lax.axis_index("seq") * group + counting(group)
    cosine, sine = phase_table(classes, counting(rows), whole, 1.0)
    real_part, imag_part = rotate(cosine[:, :, None], sine[:, :, None], real_part, imag_part)
    gathered = lax.all_to_all(
        jnp.stack([real_part, imag_part], axis=1), "seq", split_axis=3, concat_axis=2, tiled=True
    )
    cosine, sine = phase_table(counting(devices), counting(span), span, 1.0)
    inverse_scale = 1.0 / whole
    out_real = (
        jnp.einsum("ak,fkbc->fabc", cosine, gathered[:, 0], precision=HIGHEST)
        - jnp.einsum("ak,fkbc->fabc", sine, gathered[:, 1], precision=HIGHEST)
    ) * inverse_scale
    slab = lax.all_to_all(out_real, "seq", split_axis=1, concat_axis=2, tiled=True)
    return slab[:, 0]


def adjoint_spectra(spectra_real, spectra_imag, incoming_real, incoming_imag):
    toward_signal_real = spectra_real[1] * incoming_real + spectra_imag[1] * incoming_imag
    toward_signal_imag = spectra_real[1] * incoming_imag - spectra_imag[1] * incoming_real
    toward_filter_real = spectra_real[0] * incoming_real + spectra_imag[0] * incoming_imag
    toward_filter_imag = spectra_real[0] * incoming_imag - spectra_imag[0] * incoming_real
    return (toward_signal_real, toward_signal_imag, toward_filter_real, toward_filter_imag)


def shards_general(signal, filter_raw, gate, d_out, w_first, w_second):
    rows, width = signal.shape
    scale = float(rows * lax.axis_size("seq")) ** (-0.5)
    signal_wide = signal.astype(jnp.float32)
    kernel = filter_raw.astype(jnp.float32) * scale
    spectra_real, spectra_imag = forward_transform(jnp.stack([signal_wide, kernel]))
    mixed_real = spectra_real[0] * spectra_real[1] - spectra_imag[0] * spectra_imag[1]
    mixed_imag = spectra_real[0] * spectra_imag[1] + spectra_imag[0] * spectra_real[1]
    conv = inverse_transform(mixed_real[None], mixed_imag[None])[0].astype(jnp.bfloat16)
    gate_wide = gate.astype(jnp.float32)
    product = (conv.astype(jnp.float32) * gate_wide).astype(jnp.bfloat16)
    blocks = w_first.shape[0]
    block = w_first.shape[1]
    product_blocks = product.reshape(rows, blocks, block)
    first_mix = jnp.einsum(
        "tij,ijk->tik", product_blocks, w_first, preferred_element_type=jnp.float32
    ).astype(jnp.bfloat16)
    received = lax.all_to_all(first_mix, "ch", split_axis=2, concat_axis=1, tiled=True)
    incoming = d_out.reshape(rows, w_second.shape[0], w_second.shape[1])
    second_back = jnp.einsum(
        "tko,kio->tki", incoming, w_second, preferred_element_type=jnp.float32
    ).astype(jnp.bfloat16)
    grad_second = jnp.einsum("tik,tko->kio", received, incoming, preferred_element_type=jnp.float32)
    returned = lax.all_to_all(second_back, "ch", split_axis=2, concat_axis=1, tiled=True)
    grad_product = jnp.einsum(
        "tki,ijk->tij", returned, w_first, preferred_element_type=jnp.float32
    ).reshape(rows, width)
    grad_first = jnp.einsum(
        "tij,tki->ijk", product_blocks, returned, preferred_element_type=jnp.float32
    )
    grad_gate = (grad_product * conv.astype(jnp.float32)).astype(jnp.bfloat16)
    grad_conv = grad_product * gate_wide
    incoming_real, incoming_imag = forward_transform(grad_conv[None])
    sig_real, sig_imag, fil_real, fil_imag = adjoint_spectra(
        spectra_real, spectra_imag, incoming_real[0], incoming_imag[0]
    )
    results = inverse_transform(jnp.stack([sig_real, fil_real]), jnp.stack([sig_imag, fil_imag]))
    grad_signal = results[0].astype(jnp.bfloat16)
    grad_filter = (results[1] * scale).astype(jnp.bfloat16)
    grad_first = lax.psum_scatter(
        grad_first.astype(jnp.bfloat16), "seq", scatter_dimension=1, tiled=True
    ).astype(jnp.float32)
    grad_second = lax.psum_scatter(grad_second, "seq", scatter_dimension=1, tiled=True)
    return (grad_signal, grad_filter, grad_gate, grad_first, grad_second)


F32 = jnp.float32
BF16 = jnp.bfloat16
LANES = 128
HALF = 64
INNER = 128
CHUNK = 16
PARTS = 2


def dft_tables(outer, scale):
    length = outer * INNER
    q = np.arange(outer // 2 + 1)[:, None, None]
    r = np.arange(INNER)[None, :, None]
    b = np.arange(INNER)[None, None, :]
    angle = 2.0 * np.pi / length * ((b * (q + outer * r)) % length)
    c, s = np.cos(angle), np.sin(angle)
    forward = np.concatenate(
        [np.concatenate([c, s], axis=2), np.concatenate([-s, c], axis=2)], axis=1
    )
    inverse = forward.transpose(0, 2, 1) * (scale / length)
    return forward.astype(ml_dtypes.bfloat16), inverse.astype(ml_dtypes.bfloat16)


def times(value, cosine, sine):
    real, imag = value
    if imag is None:
        return (real * cosine, real * sine)
    return (real * cosine - imag * sine, real * sine + imag * cosine)


def real_dft(values, length):
    if length == 2:
        return [(values[0], None), (values[0], None)]
    even = real_dft(values[0::2], length // 2)
    odd = real_dft(values[1::2], length // 2)
    half, quarter = length // 2, length // 4
    out = [None] * (half + 1)
    for q in range(quarter + 1):
        er, ei = even[q]
        if q == 0:
            out[0] = (er + odd[0][0], None)
            out[half] = (er - odd[0][0], None)
        elif q == quarter:
            out[q] = (er, -odd[q][0])
        else:
            angle = 2.0 * math.pi * q / length
            tr, ti = times(odd[q], math.cos(angle), -math.sin(angle))
            out[q] = (er + tr, ei + ti)
            out[half - q] = (er - tr, ti - ei)
    return out


def real_inverse(values, length):
    if length == 2:
        return [values[0][0] + values[1][0]]
    half, quarter = length // 2, length // 4
    even, odd = [], []
    for q in range(quarter + 1):
        zr, zi = values[q]
        if q == 0:
            wr = values[half][0]
            even.append((zr + wr, None))
            odd.append((zr - wr, None))
        elif q == quarter:
            even.append((zr + zr, None))
            odd.append((-(zi + zi), None))
        else:
            wr, wi = values[half - q]
            even.append((zr + wr, zi - wi))
            angle = 2.0 * math.pi * q / length
            odd.append(times((zr - wr, zi + wi), math.cos(angle), math.sin(angle)))
    out = [None] * half
    out[0::2] = real_inverse(even, half)
    out[1::2] = real_inverse(odd, half)
    return out


def low_lanes(rows):
    return lax.broadcasted_iota(jnp.int32, (rows, LANES), 1) < HALF


def swap(value):
    return pltpu.roll(value, HALF, 1)


def store_classes(y_ref, rows, spectrum):
    for q, (real, imag) in enumerate(spectrum):
        y_ref[q, pl.ds(rows, CHUNK), :] = real.astype(BF16)
        imag = jnp.zeros_like(real) if imag is None else imag
        y_ref[q, pl.ds(INNER + rows, CHUNK), :] = imag.astype(BF16)


def load_classes(z_ref, rows, classes):
    out = []
    for q in range(classes):
        real = z_ref[q, pl.ds(rows, CHUNK), :]
        edge = q == 0 or q == classes - 1
        out.append((real, None if edge else z_ref[q, pl.ds(INNER + rows, CHUNK), :]))
    return out


def pack_part(signal_ref, filter_ref, out_ref, part):
    size = INNER // PARTS
    low = low_lanes(size)
    for p in range(out_ref.shape[0] // 2):
        cols = slice(p * LANES, (p + 1) * LANES)
        for m in range(signal_ref.shape[0] // INNER):
            source = slice(m * INNER + part * size, m * INNER + (part + 1) * size)
            rows = slice(m * size, (m + 1) * size)
            a = signal_ref[source, cols].astype(F32)
            b = filter_ref[source, cols].astype(F32)
            out_ref[2 * p, rows, :] = jnp.where(low, a, swap(b)).astype(BF16)
            out_ref[2 * p + 1, rows, :] = jnp.where(low, swap(a), b).astype(BF16)


def unpack_part(in_ref, signal_ref, filter_ref, part):
    size = INNER // PARTS
    low = low_lanes(size)
    for p in range(in_ref.shape[0] // 2):
        cols = slice(p * LANES, (p + 1) * LANES)
        for m in range(signal_ref.shape[0] // INNER):
            target = slice(m * INNER + part * size, m * INNER + (part + 1) * size)
            rows = slice(m * size, (m + 1) * size)
            a = in_ref[2 * p, rows, :].astype(F32)
            b = in_ref[2 * p + 1, rows, :].astype(F32)
            filter_ref[target, cols] = jnp.where(low, a, swap(b)).astype(BF16)
            signal_ref[target, cols] = jnp.where(low, swap(a), b).astype(BF16)


def conv_first(pair_ref, y_ref, part, outer):
    size = INNER // PARTS
    tiles = outer // 2 // pair_ref.shape[0]

    def first(j, carry):
        at = pl.multiple_of(j * CHUNK, CHUNK)
        points = [
            pair_ref[a // tiles, pl.ds((a % tiles) * size + at, CHUNK), :].astype(F32)
            for a in range(outer // 2)
        ]
        store_classes(y_ref, part * size + at, real_dft(points, outer))
        return carry

    lax.fori_loop(0, size // CHUNK, first, 0)


def conv_kernel(forward_ref, inverse_ref, spec_ref, conv_ref, y_ref, z_ref):
    devices, packed, _ = conv_ref.shape
    classes = forward_ref.shape[0]
    outer = 2 * (classes - 1)
    tiles = 2 * packed // INNER

    def middle(q, carry):
        x = jnp.dot(forward_ref[q], y_ref[q], preferred_element_type=F32)
        spec_ref[q] = x.astype(BF16)
        o = swap(x)
        xr, xi, orr, oi = x[:INNER], x[INNER:], o[:INNER], o[INNER:]
        mixed = jnp.concatenate([xr * orr - xi * oi, xr * oi + xi * orr], axis=0)
        z_ref[q] = jnp.dot(inverse_ref[q], mixed.astype(BF16), preferred_element_type=F32)
        return carry

    lax.fori_loop(0, classes, middle, 0, unroll=11)
    low = low_lanes(CHUNK)
    halves = tiles // 2

    def last(j, carry):
        at = pl.multiple_of(j * CHUNK, CHUNK)
        points = real_inverse(load_classes(z_ref, at, classes), outer)
        for s in range(devices):
            for m in range(halves):
                a = s * tiles + m
                value = jnp.where(low, points[a], points[a + halves])
                conv_ref[s, pl.ds(m * INNER + at, CHUNK), :] = value.astype(BF16)
        return carry

    lax.fori_loop(0, INNER // CHUNK, last, 0)


def adjoint_kernel(grad_ref, spec_ref, forward_ref, inverse_ref, y_ref, z_ref):
    devices, packed, _ = grad_ref.shape
    classes = forward_ref.shape[0]
    outer = 2 * (classes - 1)
    halves = packed // INNER
    tiles = 2 * halves
    low = low_lanes(CHUNK)

    def first(j, carry):
        at = pl.multiple_of(j * CHUNK, CHUNK)
        points = [None] * (outer // 2)
        for s in range(devices):
            for m in range(halves):
                value = grad_ref[s, pl.ds(m * INNER + at, CHUNK), :].astype(F32)
                other = swap(value)
                points[s * tiles + m] = jnp.where(low, value, other)
                points[s * tiles + halves + m] = jnp.where(low, other, value)
        store_classes(y_ref, at, real_dft(points, outer))
        return carry

    lax.fori_loop(0, INNER // CHUNK, first, 0)

    def middle(q, carry):
        g = jnp.dot(forward_ref[q], y_ref[q], preferred_element_type=F32)
        x = spec_ref[q].astype(F32)
        gr, gi, xr, xi = g[:INNER], g[INNER:], x[:INNER], x[INNER:]
        mixed = jnp.concatenate([xr * gr + xi * gi, xr * gi - xi * gr], axis=0)
        z_ref[q] = jnp.dot(inverse_ref[q], mixed.astype(BF16), preferred_element_type=F32)
        return carry

    lax.fori_loop(0, classes, middle, 0, unroll=11)


def adjoint_last(z_ref, out_ref, part):
    size = INNER // PARTS
    classes = z_ref.shape[0]
    outer = 2 * (classes - 1)
    tiles = outer // 2 // out_ref.shape[0]

    def last(j, carry):
        at = pl.multiple_of(j * CHUNK, CHUNK)
        points = real_inverse(load_classes(z_ref, part * size + at, classes), outer)
        for a in range(outer // 2):
            rows = pl.ds((a % tiles) * size + at, CHUNK)
            out_ref[a // tiles, rows, :] = points[a].astype(BF16)
        return carry

    lax.fori_loop(0, size // CHUNK, last, 0)


def joined(ref):
    return jnp.concatenate([ref[c] for c in range(ref.shape[0])], axis=1)


def grad_product_of(back, first):
    return lax.dot_general(back, first, (((1,), (1,)), ((), ())), preferred_element_type=F32)


def grad_conv_kernel(back_ref, first_ref, gate_ref, out_ref):
    value = grad_product_of(joined(back_ref), first_ref[...]) * gate_ref[...].astype(F32)
    half = value.shape[0] // 2
    low = low_lanes(half)
    for p in range(out_ref.shape[0] // 2):
        top = value[:half, p * LANES : (p + 1) * LANES]
        bottom = value[half:, p * LANES : (p + 1) * LANES]
        out_ref[2 * p] = jnp.where(low, top, swap(bottom)).astype(BF16)
        out_ref[2 * p + 1] = jnp.where(low, swap(top), bottom).astype(BF16)


def mix_kernel(conv_ref, back_ref, first_ref, gate_ref, mix_ref, grad_gate_ref, grad_first_ref):
    devices, half, _ = conv_ref.shape
    low = low_lanes(half)
    parts = []
    for p in range(devices // 2):
        a = conv_ref[2 * p].astype(F32)
        b = conv_ref[2 * p + 1].astype(F32)
        parts.append(
            jnp.concatenate([jnp.where(low, a, swap(b)), jnp.where(low, swap(a), b)], axis=0)
        )
    conv = jnp.concatenate(parts, axis=1)
    product = (conv * gate_ref[...].astype(F32)).astype(BF16)
    first = first_ref[...]
    mix = jnp.dot(product, first, preferred_element_type=F32).astype(BF16)
    groups = mix_ref.shape[0]
    for c in range(groups):
        mix_ref[c] = mix[:, c * LANES : (c + 1) * LANES]
    back = joined(back_ref)
    grad_gate_ref[...] = (grad_product_of(back, first) * conv).astype(BF16)
    whole = lax.dot_general(product, back, (((0,), (0,)), ((), ())), preferred_element_type=F32)
    count = whole.shape[0]
    lane = lax.broadcasted_iota(jnp.int32, (count, LANES), 1)
    row = lax.broadcasted_iota(jnp.int32, (count, LANES), 0)
    inner = LANES // devices
    keep = lane // inner == row // (count // devices)
    grads = jnp.zeros((count, LANES), F32)
    for c in range(groups):
        value = jnp.where(keep, whole[:, c * LANES : (c + 1) * LANES], 0.0)
        shift = inner
        while shift < LANES:
            value = value + pltpu.roll(value, shift, 1)
            shift *= 2
        grads = jnp.where((lane // inner) % groups == c, value, grads)
    block = count // devices
    piece = block // devices
    pairs = devices // 2
    small = low_lanes(piece)
    for i in range(pairs):
        for s in range(devices):
            a = grads[i * block + s * piece : i * block + (s + 1) * piece]
            k = i + pairs
            b = grads[k * block + s * piece : k * block + (s + 1) * piece]
            grad_first_ref[s, i * piece : (i + 1) * piece, :] = jnp.where(small, a, b)


def second_kernel(mix_ref, d_out_ref, grad_first_ref, out_ref, inner, width):
    groups = mix_ref.shape[0]
    devices, first_rows, _ = grad_first_ref.shape
    out_ref[:, :first_rows, :] = grad_first_ref[...]
    d_out = d_out_ref[...]
    lane = lax.broadcasted_iota(jnp.int32, (LANES, LANES), 1)
    row = lax.broadcasted_iota(jnp.int32, (LANES, LANES), 0)
    folds = LANES // width
    per = devices // groups
    slot = lax.broadcasted_iota(jnp.int32, (inner, LANES), 1) // width
    for c in range(groups):
        whole = lax.dot_general(
            mix_ref[c], d_out, (((0,), (0,)), ((), ())), preferred_element_type=F32
        )
        total = jnp.zeros((LANES, LANES), F32)
        for g in range(whole.shape[1] // LANES):
            keep = lane // width + g * folds == row % inner
            total = total + jnp.where(keep, whole[:, g * LANES : (g + 1) * LANES], 0.0)
        shift = width
        while shift < LANES:
            total = total + pltpu.roll(total, shift, 1)
            shift *= 2
        for d in range(per):
            base = d * folds * inner
            piece = jnp.zeros((inner, LANES), F32)
            for i in range(folds):
                piece = jnp.where(slot == i, total[base + i * inner : base + (i + 1) * inner], piece)
            out_ref[c * per + d, first_rows:, :] = piece


PAIR, BACK, GRAD, CONV, RESULT, MIX, SMALL = range(7)
INPUTS = 6


class Exchange:
    def __init__(self, number, axis, count, send, recv, send_sem, recv_sem):
        self.axis, self.count, self.send, self.recv = axis, count, send, recv
        self.number, self.send_sem, self.recv_sem = number, send_sem, recv_sem
        self.me = lax.axis_index(axis)

    def copy(self, peer, slot):
        return pltpu.make_async_remote_copy(
            src_ref=self.send.at[peer],
            dst_ref=self.recv.at[slot],
            send_sem=self.send_sem.at[self.number, peer],
            recv_sem=self.recv_sem.at[self.number, slot],
            device_id={self.axis: peer},
            device_id_type=pl.DeviceIdType.MESH,
        )

    def peers(self):
        half = self.count // 2
        own = half * (self.me // half)
        far = [half - own + lax.rem(self.me + d, half) for d in range(half)]
        return far + [own + lax.rem(self.me + d, half) for d in range(1, half)]

    def start(self):
        for peer in self.peers():
            self.copy(peer, self.me).start()
        self.recv[self.me] = self.send[self.me]

    def wait_recv(self):
        for peer in self.peers():
            self.copy(peer, peer).wait_recv()

    def wait_send(self):
        for peer in self.peers():
            self.copy(peer, self.me).wait_send()


def spread(values, pick):
    return jnp.dot(values, pick.astype(F32).astype(BF16), preferred_element_type=F32)


def first_matrix(w_ref, blocks, inner):
    rows, block = w_ref.shape
    shape = (block, rows)
    k = lax.broadcasted_iota(jnp.int32, shape, 0)
    col = lax.broadcasted_iota(jnp.int32, shape, 1)
    wide = spread(w_ref[...], k == (col // LANES) * inner + col % inner)
    row = lax.broadcasted_iota(jnp.int32, wide.shape, 0)
    col = lax.broadcasted_iota(jnp.int32, wide.shape, 1)
    return jnp.where(row // block == (col % LANES) // inner, wide, 0.0).astype(BF16)


def second_matrix(w_ref, inner):
    rows, width = w_ref.shape
    across = rows // inner
    r = lax.broadcasted_iota(jnp.int32, (rows, rows), 0)
    c = lax.broadcasted_iota(jnp.int32, (rows, rows), 1)
    order = (c == (r % inner) * across + r // inner).astype(F32).astype(BF16)
    turned = jnp.dot(order, w_ref[...], preferred_element_type=F32).astype(BF16)
    o = lax.broadcasted_iota(jnp.int32, (width, inner * width), 0)
    c = lax.broadcasted_iota(jnp.int32, (width, inner * width), 1)
    wide = spread(turned, o == c % width)
    row = lax.broadcasted_iota(jnp.int32, wide.shape, 0)
    col = lax.broadcasted_iota(jnp.int32, wide.shape, 1)
    return jnp.where(row % inner == col // width, wide, 0.0).astype(BF16)


def whole_kernel(
    devices,
    groups,
    blocks,
    inner,
    out_block,
    *refs,
):
    inputs, (forward_hbm, inverse_hbm) = refs[:INPUTS], refs[INPUTS : INPUTS + 2]
    refs = refs[INPUTS + 2 :]
    grad_signal_ref, grad_filter_ref, grad_gate_ref, small_ref = refs[:4]
    buffers, local, rest = refs[4:18], refs[18 : 18 + INPUTS], refs[18 + INPUTS :]
    (forward, inverse, spec, y_ref, z_ref, first, grad_first) = rest[:7]
    input_sem, send_sem, recv_sem = rest[7:]
    signal_ref, filter_ref, gate_ref, d_out_ref, w_first_ref, w_second_ref = local
    axes = ["seq", "ch", "seq", "seq", "seq", "ch", "seq"]
    counts = {"seq": devices, "ch": groups}
    exchanges = {}
    number = 0
    for n, axis in enumerate(axes):
        send, recv = buffers[2 * n], buffers[2 * n + 1]
        cut = n in (PAIR, RESULT)
        made = []
        for part in range(PARTS if cut else 1):
            ends = (send.at[part], recv.at[part]) if cut else (send, recv)
            made.append(Exchange(number, axis, counts[axis], *ends, send_sem, recv_sem))
            number += 1
        exchanges[n] = made if cut else made[0]
    copies = [
        pltpu.make_async_copy(source, target, input_sem.at[n])
        for n, (source, target) in enumerate(
            zip((*inputs, forward_hbm, inverse_hbm), (*local, forward, inverse))
        )
    ]
    barrier = pltpu.get_barrier_semaphore()
    for exchange in (exchanges[GRAD], exchanges[BACK]):
        for peer in exchange.peers():
            pl.semaphore_signal(
                barrier,
                inc=1,
                device_id={exchange.axis: peer},
                device_id_type=pl.DeviceIdType.MESH,
            )
    for copy in copies[:2]:
        copy.start()
    for copy in copies[:2]:
        copy.wait()
    pack_part(signal_ref, filter_ref, exchanges[PAIR][0].send, 0)
    pl.semaphore_wait(barrier, devices + groups - 2)
    exchanges[PAIR][0].start()
    for copy in copies[2:]:
        copy.start()
    for part in range(1, PARTS):
        pack_part(signal_ref, filter_ref, exchanges[PAIR][part].send, part)
        exchanges[PAIR][part].start()
    for copy in copies[2:INPUTS]:
        copy.wait()

    second = second_matrix(w_second_ref, inner)
    back = lax.dot_general(
        d_out_ref[...], second, (((1,), (1,)), ((), ())), preferred_element_type=F32
    ).astype(BF16)
    for c in range(groups):
        exchanges[BACK].send[c] = back[:, c * LANES : (c + 1) * LANES]
    exchanges[BACK].start()
    first[...] = first_matrix(w_first_ref, blocks, inner)
    exchanges[BACK].wait_recv()
    back_ref = exchanges[BACK].recv
    grad_conv_kernel(back_ref, first, gate_ref, exchanges[GRAD].send)
    outer = 2 * (forward.shape[0] - 1)
    exchanges[PAIR][0].wait_recv()
    conv_first(exchanges[PAIR][0].recv, y_ref, 0, outer)
    for part in range(PARTS):
        exchanges[PAIR][part].wait_send()
    exchanges[GRAD].start()
    for part in range(1, PARTS):
        exchanges[PAIR][part].wait_recv()
        conv_first(exchanges[PAIR][part].recv, y_ref, part, outer)
    for copy in copies[INPUTS:]:
        copy.wait()
    conv_kernel(forward, inverse, spec, exchanges[CONV].send, y_ref, z_ref)
    exchanges[CONV].start()
    exchanges[GRAD].wait_recv()
    adjoint_kernel(exchanges[GRAD].recv, spec, forward, inverse, y_ref, z_ref)
    for part in range(PARTS):
        adjoint_last(z_ref, exchanges[RESULT][part].send, part)
        exchanges[RESULT][part].start()
    exchanges[CONV].wait_recv()
    mix_kernel(
        exchanges[CONV].recv,
        back_ref,
        first,
        gate_ref,
        exchanges[MIX].send,
        grad_gate_ref,
        grad_first,
    )
    exchanges[MIX].start()
    exchanges[MIX].wait_recv()
    second_kernel(
        exchanges[MIX].recv, d_out_ref, grad_first, exchanges[SMALL].send, inner, out_block
    )
    exchanges[SMALL].start()
    for part in range(PARTS):
        exchanges[RESULT][part].wait_recv()
        unpack_part(exchanges[RESULT][part].recv, grad_signal_ref, grad_filter_ref, part)
    exchanges[SMALL].wait_recv()
    total = exchanges[SMALL].recv[0]
    for s in range(1, devices):
        total = total + exchanges[SMALL].recv[s]
    small_ref[...] = total
    for n in (BACK, GRAD, CONV, MIX, SMALL):
        exchanges[n].wait_send()
    for exchange in exchanges[RESULT]:
        exchange.wait_send()


def finish_kernel(
    signal_ref, filter_ref, gate_ref, small_ref, signal_out, filter_out, gate_out, first_out, second_out
):
    signal_out[...] = signal_ref[...]
    filter_out[...] = filter_ref[...]
    gate_out[...] = gate_ref[...]
    blocks, piece, block = first_out.shape
    pairs = blocks // 2
    for i in range(pairs):
        value = small_ref[i * piece : (i + 1) * piece, :]
        first_out[i] = value[:, :block]
        first_out[i + pairs] = swap(value)[:, :block]
    inner, across, width = second_out.shape
    value = small_ref[pairs * piece :, :]
    for i in range(across):
        part = value if i == 0 else pltpu.roll(value, LANES - i * width, 1)
        for k in range(inner):
            second_out[k, i : i + 1, :] = part[k : k + 1, :width]


def shards_whole(signal, filter_raw, gate, d_out, w_first, w_second):
    rows, width = signal.shape
    devices = lax.axis_size("seq")
    groups = lax.axis_size("ch")
    length = rows * devices
    outer = 2 * length // INNER
    classes = outer // 2 + 1
    forward, inverse = (jnp.asarray(t) for t in dft_tables(outer, float(length) ** (-0.5)))
    blocks, block, _ = w_first.shape
    inner, across, out_block = w_second.shape
    first_rows = blocks * (block // devices) * block // LANES
    second_rows = inner * (across // devices) * out_block // LANES
    small_rows = first_rows + second_rows
    wide = ((PARTS, devices, rows // PARTS, LANES), BF16)
    half = ((devices, rows // 2, LANES), BF16)
    mixed = ((groups, rows, LANES), BF16)
    small = ((devices, small_rows, LANES), F32)
    buffers = [
        pltpu.VMEM(*kind)
        for kind in (wide, mixed, half, half, wide, mixed, small)
        for _ in range(2)
    ]
    vmem = pl.BlockSpec(memory_space=pltpu.VMEM)
    anywhere = pl.BlockSpec(memory_space=pl.ANY)
    field = jax.ShapeDtypeStruct((rows, width), BF16)
    grad_signal, grad_filter, grad_gate, sums = pl.pallas_call(
        functools.partial(whole_kernel, devices, groups, blocks, inner, out_block),
        out_shape=(field, field, field, jax.ShapeDtypeStruct((small_rows, LANES), F32)),
        in_specs=[anywhere] * (INPUTS + 2),
        out_specs=(vmem,) * 4,
        scratch_shapes=buffers
        + [pltpu.VMEM((rows, width), BF16)] * 4
        + [
            pltpu.VMEM((blocks * block, block), BF16),
            pltpu.VMEM((inner * across, out_block), BF16),
            pltpu.VMEM(forward.shape, BF16),
            pltpu.VMEM(inverse.shape, BF16),
            pltpu.VMEM((classes, 2 * INNER, LANES), BF16),
            pltpu.VMEM((classes, 2 * INNER, LANES), BF16),
            pltpu.VMEM((classes, 2 * INNER, LANES), F32),
            pltpu.VMEM((width, width), BF16),
            pltpu.VMEM((devices, first_rows, LANES), F32),
            pltpu.SemaphoreType.DMA((INPUTS + 2,)),
            pltpu.SemaphoreType.DMA((5 + 2 * PARTS, devices)),
            pltpu.SemaphoreType.DMA((5 + 2 * PARTS, devices)),
        ],
        compiler_params=pltpu.CompilerParams(
            collective_id=0, has_side_effects=True, vmem_limit_bytes=60 * 1024 * 1024
        ),
        cost_estimate=pl.CostEstimate(
            flops=20 * 10**9, bytes_accessed=16 * 10**6, transcendentals=0
        ),
    )(
        signal,
        filter_raw,
        gate,
        d_out,
        w_first.reshape(blocks * block, block),
        w_second.reshape(inner * across, out_block),
        forward,
        inverse,
    )
    shape = jax.ShapeDtypeStruct
    return pl.pallas_call(
        finish_kernel,
        out_shape=(
            field,
            field,
            field,
            shape((blocks, block // devices, block), F32),
            shape((inner, across // devices, out_block), F32),
        ),
        compiler_params=pltpu.CompilerParams(vmem_limit_bytes=60 * 1024 * 1024),
    )(grad_signal, grad_filter, grad_gate, sums)


def shards(signal, filter_raw, gate, d_out, w_first, w_second):
    rows, width = signal.shape
    devices = lax.axis_size("seq")
    blocks, block, _ = w_first.shape
    inner, across, out_block = w_second.shape
    fits = (
        blocks == devices
        and block == HALF
        and width == devices * HALF
        and width == lax.axis_size("ch") * LANES
        and width == inner * out_block
        and blocks * inner == LANES
        and LANES // out_block == across // devices
        and lax.axis_size("ch") * inner == block
        and devices % lax.axis_size("ch") == 0
        and block // devices == 8
        and rows % (2 * INNER) == 0
        and (rows * devices // INNER) & (rows * devices // INNER - 1) == 0
    )
    body = shards_whole if fits else shards_general
    return body(signal, filter_raw, gate, d_out, w_first, w_second)


def solution(mesh):
    in_specs = (
        P("seq", "ch"),
        P("seq", "ch"),
        P("seq", "ch"),
        P("seq", "ch"),
        P("ch", None, None),
        P("ch", None, None),
    )
    out_specs = (
        P("seq", "ch"),
        P("seq", "ch"),
        P("seq", "ch"),
        P("ch", "seq", None),
        P("ch", "seq", None),
    )
    return jax.shard_map(shards, mesh=mesh, in_specs=in_specs, out_specs=out_specs, check_vma=False)
```

```python
import functools
import math

import jax
import jax.numpy as jnp
import ml_dtypes
import numpy as np
from jax import lax
from jax.experimental import pallas as pl
from jax.experimental.pallas import tpu as pltpu
from jax.sharding import PartitionSpec as P

HIGHEST = lax.Precision.HIGHEST


def counting(count):
    return jnp.arange(count, dtype=jnp.int32)


def phase_table(row_ids, col_ids, length, sign):
    angles = (
        2.0 * math.pi / length * (row_ids[:, None] * col_ids[None, :] % length).astype(jnp.float32)
    )
    return (jnp.cos(angles), sign * jnp.sin(angles))


def contract(form, table, real_part, imag_part):
    cosine, sine = table
    out_real = jnp.einsum(form, cosine, real_part, precision=HIGHEST) - jnp.einsum(
        form, sine, imag_part, precision=HIGHEST
    )
    out_imag = jnp.einsum(form, cosine, imag_part, precision=HIGHEST) + jnp.einsum(
        form, sine, real_part, precision=HIGHEST
    )
    return (out_real, out_imag)


def rotate(cosine, sine, real_part, imag_part):
    return (real_part * cosine - imag_part * sine, real_part * sine + imag_part * cosine)


def factors(length):
    return (length // 128, 128)


def local_forward(real_part, imag_part):
    fields, group, rows, width = real_part.shape
    outer, inner = factors(rows)
    real_part = real_part.reshape(fields, group, outer, inner, width)
    imag_part = imag_part.reshape(fields, group, outer, inner, width)
    real_part, imag_part = contract(
        "qa,fkabc->fkqbc",
        phase_table(counting(outer), counting(outer), outer, -1.0),
        real_part,
        imag_part,
    )
    cosine, sine = phase_table(counting(outer), counting(inner), rows, -1.0)
    real_part, imag_part = rotate(cosine[:, :, None], sine[:, :, None], real_part, imag_part)
    return contract(
        "rb,fkqbc->fkqrc",
        phase_table(counting(inner), counting(inner), inner, -1.0),
        real_part,
        imag_part,
    )


def local_inverse(real_part, imag_part):
    fields, group, outer, inner, width = real_part.shape
    rows = outer * inner
    real_part, imag_part = contract(
        "br,fkqrc->fkqbc",
        phase_table(counting(inner), counting(inner), inner, 1.0),
        real_part,
        imag_part,
    )
    cosine, sine = phase_table(counting(outer), counting(inner), rows, 1.0)
    real_part, imag_part = rotate(cosine[:, :, None], sine[:, :, None], real_part, imag_part)
    real_part, imag_part = contract(
        "aq,fkqbc->fkabc",
        phase_table(counting(outer), counting(outer), outer, 1.0),
        real_part,
        imag_part,
    )
    return (
        real_part.reshape(fields, group, rows, width),
        imag_part.reshape(fields, group, rows, width),
    )


def forward_transform(fields):
    devices = lax.axis_size("seq")
    count, rows, width = fields.shape
    piece = rows // devices
    span = 2 * devices
    whole = span * rows
    parts = lax.all_to_all(fields[:, None], "seq", split_axis=2, concat_axis=1, tiled=True)
    cosine, sine = phase_table(counting(span), counting(devices), span, -1.0)
    real_part = jnp.einsum("ka,fabc->fkbc", cosine, parts, precision=HIGHEST)
    imag_part = jnp.einsum("ka,fabc->fkbc", sine, parts, precision=HIGHEST)
    positions = lax.axis_index("seq") * piece + counting(piece)
    cosine, sine = phase_table(counting(span), positions, whole, -1.0)
    real_part, imag_part = rotate(cosine[:, :, None], sine[:, :, None], real_part, imag_part)
    spectrum = lax.all_to_all(
        jnp.stack([real_part, imag_part], axis=1), "seq", split_axis=2, concat_axis=3, tiled=True
    )
    return local_forward(spectrum[:, 0], spectrum[:, 1])


def inverse_transform(real_part, imag_part):
    devices = lax.axis_size("seq")
    real_part, imag_part = local_inverse(real_part, imag_part)
    group = real_part.shape[1]
    rows = real_part.shape[2]
    span = 2 * devices
    whole = span * rows
    classes = lax.axis_index("seq") * group + counting(group)
    cosine, sine = phase_table(classes, counting(rows), whole, 1.0)
    real_part, imag_part = rotate(cosine[:, :, None], sine[:, :, None], real_part, imag_part)
    gathered = lax.all_to_all(
        jnp.stack([real_part, imag_part], axis=1), "seq", split_axis=3, concat_axis=2, tiled=True
    )
    cosine, sine = phase_table(counting(devices), counting(span), span, 1.0)
    inverse_scale = 1.0 / whole
    out_real = (
        jnp.einsum("ak,fkbc->fabc", cosine, gathered[:, 0], precision=HIGHEST)
        - jnp.einsum("ak,fkbc->fabc", sine, gathered[:, 1], precision=HIGHEST)
    ) * inverse_scale
    slab = lax.all_to_all(out_real, "seq", split_axis=1, concat_axis=2, tiled=True)
    return slab[:, 0]


def adjoint_spectra(spectra_real, spectra_imag, incoming_real, incoming_imag):
    toward_signal_real = spectra_real[1] * incoming_real + spectra_imag[1] * incoming_imag
    toward_signal_imag = spectra_real[1] * incoming_imag - spectra_imag[1] * incoming_real
    toward_filter_real = spectra_real[0] * incoming_real + spectra_imag[0] * incoming_imag
    toward_filter_imag = spectra_real[0] * incoming_imag - spectra_imag[0] * incoming_real
    return (toward_signal_real, toward_signal_imag, toward_filter_real, toward_filter_imag)


def shards_general(signal, filter_raw, gate, d_out, w_first, w_second):
    rows, width = signal.shape
    scale = float(rows * lax.axis_size("seq")) ** (-0.5)
    signal_wide = signal.astype(jnp.float32)
    kernel = filter_raw.astype(jnp.float32) * scale
    spectra_real, spectra_imag = forward_transform(jnp.stack([signal_wide, kernel]))
    mixed_real = spectra_real[0] * spectra_real[1] - spectra_imag[0] * spectra_imag[1]
    mixed_imag = spectra_real[0] * spectra_imag[1] + spectra_imag[0] * spectra_real[1]
    conv = inverse_transform(mixed_real[None], mixed_imag[None])[0].astype(jnp.bfloat16)
    gate_wide = gate.astype(jnp.float32)
    product = (conv.astype(jnp.float32) * gate_wide).astype(jnp.bfloat16)
    blocks = w_first.shape[0]
    block = w_first.shape[1]
    product_blocks = product.reshape(rows, blocks, block)
    first_mix = jnp.einsum(
        "tij,ijk->tik", product_blocks, w_first, preferred_element_type=jnp.float32
    ).astype(jnp.bfloat16)
    received = lax.all_to_all(first_mix, "ch", split_axis=2, concat_axis=1, tiled=True)
    incoming = d_out.reshape(rows, w_second.shape[0], w_second.shape[1])
    second_back = jnp.einsum(
        "tko,kio->tki", incoming, w_second, preferred_element_type=jnp.float32
    ).astype(jnp.bfloat16)
    grad_second = jnp.einsum("tik,tko->kio", received, incoming, preferred_element_type=jnp.float32)
    returned = lax.all_to_all(second_back, "ch", split_axis=2, concat_axis=1, tiled=True)
    grad_product = jnp.einsum(
        "tki,ijk->tij", returned, w_first, preferred_element_type=jnp.float32
    ).reshape(rows, width)
    grad_first = jnp.einsum(
        "tij,tki->ijk", product_blocks, returned, preferred_element_type=jnp.float32
    )
    grad_gate = (grad_product * conv.astype(jnp.float32)).astype(jnp.bfloat16)
    grad_conv = grad_product * gate_wide
    incoming_real, incoming_imag = forward_transform(grad_conv[None])
    sig_real, sig_imag, fil_real, fil_imag = adjoint_spectra(
        spectra_real, spectra_imag, incoming_real[0], incoming_imag[0]
    )
    results = inverse_transform(jnp.stack([sig_real, fil_real]), jnp.stack([sig_imag, fil_imag]))
    grad_signal = results[0].astype(jnp.bfloat16)
    grad_filter = (results[1] * scale).astype(jnp.bfloat16)
    grad_first = lax.psum_scatter(
        grad_first.astype(jnp.bfloat16), "seq", scatter_dimension=1, tiled=True
    ).astype(jnp.float32)
    grad_second = lax.psum_scatter(grad_second, "seq", scatter_dimension=1, tiled=True)
    return (grad_signal, grad_filter, grad_gate, grad_first, grad_second)


F32 = jnp.float32
BF16 = jnp.bfloat16
LANES = 128
HALF = 64
INNER = 128
CHUNK = 16
PARTS = 2


def dft_tables(outer, scale):
    length = outer * INNER
    q = np.arange(outer // 2 + 1)[:, None, None]
    r = np.arange(INNER)[None, :, None]
    b = np.arange(INNER)[None, None, :]
    angle = 2.0 * np.pi / length * ((b * (q + outer * r)) % length)
    c, s = np.cos(angle), np.sin(angle)
    forward = np.concatenate(
        [np.concatenate([c, s], axis=2), np.concatenate([-s, c], axis=2)], axis=1
    )
    inverse = forward.transpose(0, 2, 1) * (scale / length)
    return forward.astype(ml_dtypes.bfloat16), inverse.astype(ml_dtypes.bfloat16)


def times(value, cosine, sine):
    real, imag = value
    if imag is None:
        return (real * cosine, real * sine)
    return (real * cosine - imag * sine, real * sine + imag * cosine)


def real_dft(values, length):
    if length == 2:
        return [(values[0], None), (values[0], None)]
    even = real_dft(values[0::2], length // 2)
    odd = real_dft(values[1::2], length // 2)
    half, quarter = length // 2, length // 4
    out = [None] * (half + 1)
    for q in range(quarter + 1):
        er, ei = even[q]
        if q == 0:
            out[0] = (er + odd[0][0], None)
            out[half] = (er - odd[0][0], None)
        elif q == quarter:
            out[q] = (er, -odd[q][0])
        else:
            angle = 2.0 * math.pi * q / length
            tr, ti = times(odd[q], math.cos(angle), -math.sin(angle))
            out[q] = (er + tr, ei + ti)
            out[half - q] = (er - tr, ti - ei)
    return out


def real_inverse(values, length):
    if length == 2:
        return [values[0][0] + values[1][0]]
    half, quarter = length // 2, length // 4
    even, odd = [], []
    for q in range(quarter + 1):
        zr, zi = values[q]
        if q == 0:
            wr = values[half][0]
            even.append((zr + wr, None))
            odd.append((zr - wr, None))
        elif q == quarter:
            even.append((zr + zr, None))
            odd.append((-(zi + zi), None))
        else:
            wr, wi = values[half - q]
            even.append((zr + wr, zi - wi))
            angle = 2.0 * math.pi * q / length
            odd.append(times((zr - wr, zi + wi), math.cos(angle), math.sin(angle)))
    out = [None] * half
    out[0::2] = real_inverse(even, half)
    out[1::2] = real_inverse(odd, half)
    return out


def low_lanes(rows):
    return lax.broadcasted_iota(jnp.int32, (rows, LANES), 1) < HALF


def swap(value):
    return pltpu.roll(value, HALF, 1)


def store_classes(y_ref, rows, spectrum):
    for q, (real, imag) in enumerate(spectrum):
        y_ref[q, pl.ds(rows, CHUNK), :] = real.astype(BF16)
        imag = jnp.zeros_like(real) if imag is None else imag
        y_ref[q, pl.ds(INNER + rows, CHUNK), :] = imag.astype(BF16)


def load_classes(z_ref, rows, classes):
    out = []
    for q in range(classes):
        real = z_ref[q, pl.ds(rows, CHUNK), :]
        edge = q == 0 or q == classes - 1
        out.append((real, None if edge else z_ref[q, pl.ds(INNER + rows, CHUNK), :]))
    return out


def pack_part(signal_ref, filter_ref, out_ref, part):
    size = INNER // PARTS
    low = low_lanes(size)
    for p in range(out_ref.shape[0] // 2):
        cols = slice(p * LANES, (p + 1) * LANES)
        for m in range(signal_ref.shape[0] // INNER):
            source = slice(m * INNER + part * size, m * INNER + (part + 1) * size)
            rows = slice(m * size, (m + 1) * size)
            a = signal_ref[source, cols].astype(F32)
            b = filter_ref[source, cols].astype(F32)
            out_ref[2 * p, rows, :] = jnp.where(low, a, swap(b)).astype(BF16)
            out_ref[2 * p + 1, rows, :] = jnp.where(low, swap(a), b).astype(BF16)


def unpack_part(in_ref, signal_ref, filter_ref, part):
    size = INNER // PARTS
    low = low_lanes(size)
    for p in range(in_ref.shape[0] // 2):
        cols = slice(p * LANES, (p + 1) * LANES)
        for m in range(signal_ref.shape[0] // INNER):
            target = slice(m * INNER + part * size, m * INNER + (part + 1) * size)
            rows = slice(m * size, (m + 1) * size)
            a = in_ref[2 * p, rows, :].astype(F32)
            b = in_ref[2 * p + 1, rows, :].astype(F32)
            filter_ref[target, cols] = jnp.where(low, a, swap(b)).astype(BF16)
            signal_ref[target, cols] = jnp.where(low, swap(a), b).astype(BF16)


def conv_first(pair_ref, y_ref, part, outer):
    size = INNER // PARTS
    tiles = outer // 2 // pair_ref.shape[0]

    def first(j, carry):
        at = pl.multiple_of(j * CHUNK, CHUNK)
        points = [
            pair_ref[a // tiles, pl.ds((a % tiles) * size + at, CHUNK), :].astype(F32)
            for a in range(outer // 2)
        ]
        store_classes(y_ref, part * size + at, real_dft(points, outer))
        return carry

    lax.fori_loop(0, size // CHUNK, first, 0)


def conv_kernel(forward_ref, inverse_ref, spec_ref, conv_ref, y_ref, z_ref):
    devices, packed, _ = conv_ref.shape
    classes = forward_ref.shape[0]
    outer = 2 * (classes - 1)
    tiles = 2 * packed // INNER

    def middle(q, carry):
        x = jnp.dot(forward_ref[q], y_ref[q], preferred_element_type=F32)
        spec_ref[q] = x.astype(BF16)
        o = swap(x)
        xr, xi, orr, oi = x[:INNER], x[INNER:], o[:INNER], o[INNER:]
        mixed = jnp.concatenate([xr * orr - xi * oi, xr * oi + xi * orr], axis=0)
        z_ref[q] = jnp.dot(inverse_ref[q], mixed.astype(BF16), preferred_element_type=F32)
        return carry

    lax.fori_loop(0, classes, middle, 0, unroll=11)
    low = low_lanes(CHUNK)
    halves = tiles // 2

    def last(j, carry):
        at = pl.multiple_of(j * CHUNK, CHUNK)
        points = real_inverse(load_classes(z_ref, at, classes), outer)
        for s in range(devices):
            for m in range(halves):
                a = s * tiles + m
                value = jnp.where(low, points[a], points[a + halves])
                conv_ref[s, pl.ds(m * INNER + at, CHUNK), :] = value.astype(BF16)
        return carry

    lax.fori_loop(0, INNER // CHUNK, last, 0)


def adjoint_kernel(grad_ref, spec_ref, forward_ref, inverse_ref, y_ref, z_ref):
    devices, packed, _ = grad_ref.shape
    classes = forward_ref.shape[0]
    outer = 2 * (classes - 1)
    halves = packed // INNER
    tiles = 2 * halves
    low = low_lanes(CHUNK)

    def first(j, carry):
        at = pl.multiple_of(j * CHUNK, CHUNK)
        points = [None] * (outer // 2)
        for s in range(devices):
            for m in range(halves):
                value = grad_ref[s, pl.ds(m * INNER + at, CHUNK), :].astype(F32)
                other = swap(value)
                points[s * tiles + m] = jnp.where(low, value, other)
                points[s * tiles + halves + m] = jnp.where(low, other, value)
        store_classes(y_ref, at, real_dft(points, outer))
        return carry

    lax.fori_loop(0, INNER // CHUNK, first, 0)

    def middle(q, carry):
        g = jnp.dot(forward_ref[q], y_ref[q], preferred_element_type=F32)
        x = spec_ref[q].astype(F32)
        gr, gi, xr, xi = g[:INNER], g[INNER:], x[:INNER], x[INNER:]
        mixed = jnp.concatenate([xr * gr + xi * gi, xr * gi - xi * gr], axis=0)
        z_ref[q] = jnp.dot(inverse_ref[q], mixed.astype(BF16), preferred_element_type=F32)
        return carry

    lax.fori_loop(0, classes, middle, 0, unroll=11)


def adjoint_last(z_ref, out_ref, part):
    size = INNER // PARTS
    classes = z_ref.shape[0]
    outer = 2 * (classes - 1)
    tiles = outer // 2 // out_ref.shape[0]

    def last(j, carry):
        at = pl.multiple_of(j * CHUNK, CHUNK)
        points = real_inverse(load_classes(z_ref, part * size + at, classes), outer)
        for a in range(outer // 2):
            rows = pl.ds((a % tiles) * size + at, CHUNK)
            out_ref[a // tiles, rows, :] = points[a].astype(BF16)
        return carry

    lax.fori_loop(0, size // CHUNK, last, 0)


def joined(ref):
    return jnp.concatenate([ref[c] for c in range(ref.shape[0])], axis=1)


def grad_product_of(back, first):
    return lax.dot_general(back, first, (((1,), (1,)), ((), ())), preferred_element_type=F32)


def grad_conv_kernel(back_ref, first_ref, gate_ref, out_ref):
    value = grad_product_of(joined(back_ref), first_ref[...]) * gate_ref[...].astype(F32)
    half = value.shape[0] // 2
    low = low_lanes(half)
    for p in range(out_ref.shape[0] // 2):
        top = value[:half, p * LANES : (p + 1) * LANES]
        bottom = value[half:, p * LANES : (p + 1) * LANES]
        out_ref[2 * p] = jnp.where(low, top, swap(bottom)).astype(BF16)
        out_ref[2 * p + 1] = jnp.where(low, swap(top), bottom).astype(BF16)


def mix_kernel(conv_ref, back_ref, first_ref, gate_ref, mix_ref, grad_gate_ref, grad_first_ref):
    devices, half, _ = conv_ref.shape
    low = low_lanes(half)
    parts = []
    for p in range(devices // 2):
        a = conv_ref[2 * p].astype(F32)
        b = conv_ref[2 * p + 1].astype(F32)
        parts.append(
            jnp.concatenate([jnp.where(low, a, swap(b)), jnp.where(low, swap(a), b)], axis=0)
        )
    conv = jnp.concatenate(parts, axis=1)
    product = (conv * gate_ref[...].astype(F32)).astype(BF16)
    first = first_ref[...]
    mix = jnp.dot(product, first, preferred_element_type=F32).astype(BF16)
    groups = mix_ref.shape[0]
    for c in range(groups):
        mix_ref[c] = mix[:, c * LANES : (c + 1) * LANES]
    back = joined(back_ref)
    grad_gate_ref[...] = (grad_product_of(back, first) * conv).astype(BF16)
    whole = lax.dot_general(product, back, (((0,), (0,)), ((), ())), preferred_element_type=F32)
    count = whole.shape[0]
    lane = lax.broadcasted_iota(jnp.int32, (count, LANES), 1)
    row = lax.broadcasted_iota(jnp.int32, (count, LANES), 0)
    inner = LANES // devices
    keep = lane // inner == row // (count // devices)
    grads = jnp.zeros((count, LANES), F32)
    for c in range(groups):
        value = jnp.where(keep, whole[:, c * LANES : (c + 1) * LANES], 0.0)
        shift = inner
        while shift < LANES:
            value = value + pltpu.roll(value, shift, 1)
            shift *= 2
        grads = jnp.where((lane // inner) % groups == c, value, grads)
    block = count // devices
    piece = block // devices
    pairs = devices // 2
    small = low_lanes(piece)
    for i in range(pairs):
        for s in range(devices):
            a = grads[i * block + s * piece : i * block + (s + 1) * piece]
            k = i + pairs
            b = grads[k * block + s * piece : k * block + (s + 1) * piece]
            grad_first_ref[s, i * piece : (i + 1) * piece, :] = jnp.where(small, a, b)


def second_kernel(mix_ref, d_out_ref, grad_first_ref, out_ref, inner, width):
    groups = mix_ref.shape[0]
    devices, first_rows, _ = grad_first_ref.shape
    out_ref[:, :first_rows, :] = grad_first_ref[...]
    d_out = d_out_ref[...]
    lane = lax.broadcasted_iota(jnp.int32, (LANES, LANES), 1)
    row = lax.broadcasted_iota(jnp.int32, (LANES, LANES), 0)
    folds = LANES // width
    per = devices // groups
    slot = lax.broadcasted_iota(jnp.int32, (inner, LANES), 1) // width
    for c in range(groups):
        whole = lax.dot_general(
            mix_ref[c], d_out, (((0,), (0,)), ((), ())), preferred_element_type=F32
        )
        total = jnp.zeros((LANES, LANES), F32)
        for g in range(whole.shape[1] // LANES):
            keep = lane // width + g * folds == row % inner
            total = total + jnp.where(keep, whole[:, g * LANES : (g + 1) * LANES], 0.0)
        shift = width
        while shift < LANES:
            total = total + pltpu.roll(total, shift, 1)
            shift *= 2
        for d in range(per):
            base = d * folds * inner
            piece = jnp.zeros((inner, LANES), F32)
            for i in range(folds):
                piece = jnp.where(slot == i, total[base + i * inner : base + (i + 1) * inner], piece)
            out_ref[c * per + d, first_rows:, :] = piece


PAIR, BACK, GRAD, CONV, RESULT, MIX, SMALL = range(7)
INPUTS = 6


class Exchange:
    def __init__(self, number, axis, count, send, recv, send_sem, recv_sem):
        self.axis, self.count, self.send, self.recv = axis, count, send, recv
        self.number, self.send_sem, self.recv_sem = number, send_sem, recv_sem
        self.me = lax.axis_index(axis)

    def copy(self, peer, slot):
        return pltpu.make_async_remote_copy(
            src_ref=self.send.at[peer],
            dst_ref=self.recv.at[slot],
            send_sem=self.send_sem.at[self.number, peer],
            recv_sem=self.recv_sem.at[self.number, slot],
            device_id={self.axis: peer},
            device_id_type=pl.DeviceIdType.MESH,
        )

    def peers(self):
        half = self.count // 2
        own = half * (self.me // half)
        far = [half - own + lax.rem(self.me + d, half) for d in range(half)]
        return far + [own + lax.rem(self.me + d, half) for d in range(1, half)]

    def start(self):
        for peer in self.peers():
            self.copy(peer, self.me).start()
        self.recv[self.me] = self.send[self.me]

    def wait_recv(self):
        for peer in self.peers():
            self.copy(peer, peer).wait_recv()

    def wait_send(self):
        for peer in self.peers():
            self.copy(peer, self.me).wait_send()


def spread(values, pick):
    return jnp.dot(values, pick.astype(F32).astype(BF16), preferred_element_type=F32)


def first_matrix(w_ref, blocks, inner):
    rows, block = w_ref.shape
    shape = (block, rows)
    k = lax.broadcasted_iota(jnp.int32, shape, 0)
    col = lax.broadcasted_iota(jnp.int32, shape, 1)
    wide = spread(w_ref[...], k == (col // LANES) * inner + col % inner)
    row = lax.broadcasted_iota(jnp.int32, wide.shape, 0)
    col = lax.broadcasted_iota(jnp.int32, wide.shape, 1)
    return jnp.where(row // block == (col % LANES) // inner, wide, 0.0).astype(BF16)


def second_matrix(w_ref, inner):
    rows, width = w_ref.shape
    across = rows // inner
    r = lax.broadcasted_iota(jnp.int32, (rows, rows), 0)
    c = lax.broadcasted_iota(jnp.int32, (rows, rows), 1)
    order = (c == (r % inner) * across + r // inner).astype(F32).astype(BF16)
    turned = jnp.dot(order, w_ref[...], preferred_element_type=F32).astype(BF16)
    o = lax.broadcasted_iota(jnp.int32, (width, inner * width), 0)
    c = lax.broadcasted_iota(jnp.int32, (width, inner * width), 1)
    wide = spread(turned, o == c % width)
    row = lax.broadcasted_iota(jnp.int32, wide.shape, 0)
    col = lax.broadcasted_iota(jnp.int32, wide.shape, 1)
    return jnp.where(row % inner == col // width, wide, 0.0).astype(BF16)


def whole_kernel(
    devices,
    groups,
    blocks,
    inner,
    out_block,
    *refs,
):
    inputs, (forward_hbm, inverse_hbm) = refs[:INPUTS], refs[INPUTS : INPUTS + 2]
    refs = refs[INPUTS + 2 :]
    grad_signal_ref, grad_filter_ref, grad_gate_ref, small_ref = refs[:4]
    buffers, local, rest = refs[4:18], refs[18 : 18 + INPUTS], refs[18 + INPUTS :]
    (forward, inverse, spec, y_ref, z_ref, first, grad_first) = rest[:7]
    input_sem, send_sem, recv_sem = rest[7:]
    signal_ref, filter_ref, gate_ref, d_out_ref, w_first_ref, w_second_ref = local
    axes = ["seq", "ch", "seq", "seq", "seq", "ch", "seq"]
    counts = {"seq": devices, "ch": groups}
    exchanges = {}
    number = 0
    for n, axis in enumerate(axes):
        send, recv = buffers[2 * n], buffers[2 * n + 1]
        cut = n in (PAIR, RESULT)
        made = []
        for part in range(PARTS if cut else 1):
            ends = (send.at[part], recv.at[part]) if cut else (send, recv)
            made.append(Exchange(number, axis, counts[axis], *ends, send_sem, recv_sem))
            number += 1
        exchanges[n] = made if cut else made[0]
    copies = [
        pltpu.make_async_copy(source, target, input_sem.at[n])
        for n, (source, target) in enumerate(
            zip((*inputs, forward_hbm, inverse_hbm), (*local, forward, inverse))
        )
    ]
    barrier = pltpu.get_barrier_semaphore()
    for exchange in (exchanges[GRAD], exchanges[BACK]):
        for peer in exchange.peers():
            pl.semaphore_signal(
                barrier,
                inc=1,
                device_id={exchange.axis: peer},
                device_id_type=pl.DeviceIdType.MESH,
            )
    for copy in copies[:2]:
        copy.start()
    for copy in copies[:2]:
        copy.wait()
    pack_part(signal_ref, filter_ref, exchanges[PAIR][0].send, 0)
    pl.semaphore_wait(barrier, devices + groups - 2)
    exchanges[PAIR][0].start()
    for copy in copies[2:]:
        copy.start()
    for part in range(1, PARTS):
        pack_part(signal_ref, filter_ref, exchanges[PAIR][part].send, part)
        exchanges[PAIR][part].start()
    for copy in copies[2:INPUTS]:
        copy.wait()

    second = second_matrix(w_second_ref, inner)
    back = lax.dot_general(
        d_out_ref[...], second, (((1,), (1,)), ((), ())), preferred_element_type=F32
    ).astype(BF16)
    for c in range(groups):
        exchanges[BACK].send[c] = back[:, c * LANES : (c + 1) * LANES]
    exchanges[BACK].start()
    first[...] = first_matrix(w_first_ref, blocks, inner)
    exchanges[BACK].wait_recv()
    back_ref = exchanges[BACK].recv
    grad_conv_kernel(back_ref, first, gate_ref, exchanges[GRAD].send)
    outer = 2 * (forward.shape[0] - 1)
    exchanges[PAIR][0].wait_recv()
    conv_first(exchanges[PAIR][0].recv, y_ref, 0, outer)
    exchanges[PAIR][0].wait_send()
    exchanges[GRAD].start()
    for part in range(1, PARTS):
        exchanges[PAIR][part].wait_recv()
        conv_first(exchanges[PAIR][part].recv, y_ref, part, outer)
    for copy in copies[INPUTS:]:
        copy.wait()
    conv_kernel(forward, inverse, spec, exchanges[CONV].send, y_ref, z_ref)
    exchanges[CONV].start()
    exchanges[GRAD].wait_recv()
    adjoint_kernel(exchanges[GRAD].recv, spec, forward, inverse, y_ref, z_ref)
    for part in range(PARTS):
        adjoint_last(z_ref, exchanges[RESULT][part].send, part)
        exchanges[RESULT][part].start()
    exchanges[CONV].wait_recv()
    mix_kernel(
        exchanges[CONV].recv,
        back_ref,
        first,
        gate_ref,
        exchanges[MIX].send,
        grad_gate_ref,
        grad_first,
    )
    exchanges[MIX].start()
    exchanges[MIX].wait_recv()
    second_kernel(
        exchanges[MIX].recv, d_out_ref, grad_first, exchanges[SMALL].send, inner, out_block
    )
    exchanges[SMALL].start()
    for part in range(PARTS):
        exchanges[RESULT][part].wait_recv()
        unpack_part(exchanges[RESULT][part].recv, grad_signal_ref, grad_filter_ref, part)
    exchanges[SMALL].wait_recv()
    total = exchanges[SMALL].recv[0]
    for s in range(1, devices):
        total = total + exchanges[SMALL].recv[s]
    small_ref[...] = total
    for n in (BACK, GRAD, CONV, MIX, SMALL):
        exchanges[n].wait_send()
    for exchange in exchanges[PAIR][1:] + exchanges[RESULT]:
        exchange.wait_send()


def finish_kernel(
    signal_ref, filter_ref, gate_ref, small_ref, signal_out, filter_out, gate_out, first_out, second_out
):
    signal_out[...] = signal_ref[...]
    filter_out[...] = filter_ref[...]
    gate_out[...] = gate_ref[...]
    blocks, piece, block = first_out.shape
    pairs = blocks // 2
    for i in range(pairs):
        value = small_ref[i * piece : (i + 1) * piece, :]
        first_out[i] = value[:, :block]
        first_out[i + pairs] = swap(value)[:, :block]
    inner, across, width = second_out.shape
    value = small_ref[pairs * piece :, :]
    for i in range(across):
        part = value if i == 0 else pltpu.roll(value, LANES - i * width, 1)
        for k in range(inner):
            second_out[k, i : i + 1, :] = part[k : k + 1, :width]


def shards_whole(signal, filter_raw, gate, d_out, w_first, w_second):
    rows, width = signal.shape
    devices = lax.axis_size("seq")
    groups = lax.axis_size("ch")
    length = rows * devices
    outer = 2 * length // INNER
    classes = outer // 2 + 1
    forward, inverse = (jnp.asarray(t) for t in dft_tables(outer, float(length) ** (-0.5)))
    blocks, block, _ = w_first.shape
    inner, across, out_block = w_second.shape
    first_rows = blocks * (block // devices) * block // LANES
    second_rows = inner * (across // devices) * out_block // LANES
    small_rows = first_rows + second_rows
    wide = ((PARTS, devices, rows // PARTS, LANES), BF16)
    half = ((devices, rows // 2, LANES), BF16)
    mixed = ((groups, rows, LANES), BF16)
    small = ((devices, small_rows, LANES), F32)
    buffers = [
        pltpu.VMEM(*kind)
        for kind in (wide, mixed, half, half, wide, mixed, small)
        for _ in range(2)
    ]
    vmem = pl.BlockSpec(memory_space=pltpu.VMEM)
    anywhere = pl.BlockSpec(memory_space=pl.ANY)
    field = jax.ShapeDtypeStruct((rows, width), BF16)
    grad_signal, grad_filter, grad_gate, sums = pl.pallas_call(
        functools.partial(whole_kernel, devices, groups, blocks, inner, out_block),
        out_shape=(field, field, field, jax.ShapeDtypeStruct((small_rows, LANES), F32)),
        in_specs=[anywhere] * (INPUTS + 2),
        out_specs=(vmem,) * 4,
        scratch_shapes=buffers
        + [pltpu.VMEM((rows, width), BF16)] * 4
        + [
            pltpu.VMEM((blocks * block, block), BF16),
            pltpu.VMEM((inner * across, out_block), BF16),
            pltpu.VMEM(forward.shape, BF16),
            pltpu.VMEM(inverse.shape, BF16),
            pltpu.VMEM((classes, 2 * INNER, LANES), BF16),
            pltpu.VMEM((classes, 2 * INNER, LANES), BF16),
            pltpu.VMEM((classes, 2 * INNER, LANES), F32),
            pltpu.VMEM((width, width), BF16),
            pltpu.VMEM((devices, first_rows, LANES), F32),
            pltpu.SemaphoreType.DMA((INPUTS + 2,)),
            pltpu.SemaphoreType.DMA((5 + 2 * PARTS, devices)),
            pltpu.SemaphoreType.DMA((5 + 2 * PARTS, devices)),
        ],
        compiler_params=pltpu.CompilerParams(
            collective_id=0, has_side_effects=True, vmem_limit_bytes=60 * 1024 * 1024
        ),
        cost_estimate=pl.CostEstimate(
            flops=20 * 10**9, bytes_accessed=16 * 10**6, transcendentals=0
        ),
    )(
        signal,
        filter_raw,
        gate,
        d_out,
        w_first.reshape(blocks * block, block),
        w_second.reshape(inner * across, out_block),
        forward,
        inverse,
    )
    shape = jax.ShapeDtypeStruct
    return pl.pallas_call(
        finish_kernel,
        out_shape=(
            field,
            field,
            field,
            shape((blocks, block // devices, block), F32),
            shape((inner, across // devices, out_block), F32),
        ),
        compiler_params=pltpu.CompilerParams(vmem_limit_bytes=60 * 1024 * 1024),
    )(grad_signal, grad_filter, grad_gate, sums)


def shards(signal, filter_raw, gate, d_out, w_first, w_second):
    rows, width = signal.shape
    devices = lax.axis_size("seq")
    blocks, block, _ = w_first.shape
    inner, across, out_block = w_second.shape
    fits = (
        blocks == devices
        and block == HALF
        and width == devices * HALF
        and width == lax.axis_size("ch") * LANES
        and width == inner * out_block
        and blocks * inner == LANES
        and LANES // out_block == across // devices
        and lax.axis_size("ch") * inner == block
        and devices % lax.axis_size("ch") == 0
        and block // devices == 8
        and rows % (2 * INNER) == 0
        and (rows * devices // INNER) & (rows * devices // INNER - 1) == 0
    )
    body = shards_whole if fits else shards_general
    return body(signal, filter_raw, gate, d_out, w_first, w_second)


def solution(mesh):
    in_specs = (
        P("seq", "ch"),
        P("seq", "ch"),
        P("seq", "ch"),
        P("seq", "ch"),
        P("ch", None, None),
        P("ch", None, None),
    )
    out_specs = (
        P("seq", "ch"),
        P("seq", "ch"),
        P("seq", "ch"),
        P("ch", "seq", None),
        P("ch", "seq", None),
    )
    return jax.shard_map(shards, mesh=mesh, in_specs=in_specs, out_specs=out_specs, check_vma=False)
```
